32 devices in a mesh: seq: 8 (over z, x), head: 4 (over y, core).
Axes of the slice: x: 2, y: 2, z: 4, core: 2. Of those that a mesh axis runs over, the one named last changes fastest.
Arguments:
- queries: bfloat16 [2048, 32, 128], P('seq', 'head')
- keys: bfloat16 [2048, 4, 128], P('seq', 'head')
- block_order: int32 [32], P('seq'), may hold values from 0 to 31, each once
- gate_query: bfloat16 [4, 128, 128], P('head'), may hold values from -0.5 to 0.5
- gate_key: bfloat16 [4, 384, 128], P('head'), may hold values from -0.3125 to 0.3125
Outputs:
- loss: float32 [], replicated
- grad_query: float32 [4, 128, 128], P('head')
- grad_key: float32 [4, 384, 128], P('head')
The draws below stay inside these ranges and needn't reach their ends.
Inputs may be any that keep to these rules, and one draw needn't show every extreme that they name: `block_order`: each block position appears exactly once.
All inputs are finite; a program needn't handle non-finite values.
Results may differ from the reference program's by a relative error of at most 0.0029.
Values may be sent and summed in bfloat16 or wider, within the bound.
A program may use at most 64 MiB of HBM per device.

```python
import jax
import jax.numpy as jnp
from jax import lax

HD = 128
GROUP = 8
BLOCK = 64
DG = 128
KVH = 4
QH = 32
S = 2048
NB = 32


def shared_keys(key):
    return jnp.clip(jax.random.normal(key, (S, KVH, HD), jnp.float32), -6.0, 6.0)


def draw_keys(key, part):
    return shared_keys(key).astype(jnp.bfloat16)


def draw_queries(key, part):
    key = jax.random.fold_in(key, 7)
    drawn = jnp.clip(jax.random.normal(key, (S, QH, HD), jnp.float32), -6.0, 6.0)
    return drawn.astype(jnp.bfloat16)


def levels(stream_key, dims, shards, low, largest):
    def one(axis_at, blocks):
        draws = jax.random.uniform(jax.random.fold_in(jax.random.fold_in(stream_key, 6), axis_at), (blocks,), jnp.float32, low / len(shards), largest / len(shards))
        return jnp.repeat(jnp.exp(draws), dims[axis_at] // blocks).reshape((-1,) + (1,) * (len(dims) - axis_at - 1))

    factor_of = one(*shards[0])
    for cut in shards[1:]:
        factor_of = factor_of * one(*cut)
    return factor_of


def scatter_about(key, shape, spread, most, shards=(), held_as=jnp.bfloat16):
    factor_of = levels(key, shape, shards, -0.22, 0.18) if shards else 1.0
    array = jax.random.normal(key, shape, jnp.float32) * spread * factor_of
    return jnp.minimum(jnp.maximum(array, -most), most).astype(held_as)


def setup_inputs(seed: int = 0) -> dict:
    splits = jax.random.split(jax.random.key(seed), 6)
    return {
        "queries": draw_queries(jax.random.fold_in(splits[5], 71), 0),
        "keys": draw_keys(jax.random.fold_in(splits[5], 71), 0),
        "block_order": jax.random.permutation(splits[2], NB).astype(jnp.int32),
        "gate_query": scatter_about(splits[3], (KVH, HD, DG), HD ** -0.5, 0.5, ((0, 4),)),
        "gate_key": scatter_about(splits[4], (KVH, 3 * HD, DG), (3 * HD) ** -0.5, 0.3125, ((0, 4),)),
    }


HIGH = lax.Precision.HIGHEST

def pooled_targets(queries, keys, block_order):
    span = 512
    nch = S // span
    offs = jnp.arange(BLOCK, dtype=jnp.int32)
    pos = (block_order[:, None] * BLOCK + offs[None, :]).reshape(S)
    scale = HD ** (-0.5)

    def one(index):
        kvh = index // nch
        part = index % nch
        qs = lax.dynamic_slice(queries, (part * span, kvh * GROUP, jnp.int32(0)), (span, GROUP, HD))
        ks = lax.dynamic_index_in_dim(keys, kvh, 1, keepdims=False)
        qpos = lax.dynamic_slice_in_dim(pos, part * span, span, 0)
        scores = jnp.einsum('tgd,ud->gtu', qs.astype(jnp.float32), ks.astype(jnp.float32)) * scale
        scores = jnp.where(pos[None, None, :] > qpos[None, :, None], -1e+30, scores)
        rmax = lax.optimization_barrier(jnp.max(scores, axis=-1))
        lse = rmax + jnp.log(lax.optimization_barrier(jnp.sum(jnp.exp(scores - rmax[..., None]), axis=-1)))
        bmax = lax.optimization_barrier(jnp.max(scores.reshape(GROUP, span, NB, BLOCK), axis=-1))
        probs = jnp.exp(bmax - lse[..., None])
        return lax.optimization_barrier(jnp.max(probs.reshape(GROUP, span // BLOCK, BLOCK, NB), axis=2))
    out = lax.map(one, jnp.arange(KVH * nch, dtype=jnp.int32))
    out = out.reshape(KVH, nch, GROUP, span // BLOCK, NB).transpose(0, 2, 1, 3, 4).reshape(QH, NB, NB)
    return out / lax.optimization_barrier(jnp.sum(out, axis=-1, keepdims=True))

def reference(queries, keys, block_order, gate_query, gate_key):
    target = pooled_targets(queries, keys, block_order)
    qpool = lax.optimization_barrier(jnp.mean(queries.reshape(NB, BLOCK, QH, HD).astype(jnp.float32), axis=1)).astype(jnp.bfloat16)
    kb = keys.reshape(NB, BLOCK, KVH, HD)
    kmean = lax.optimization_barrier(jnp.mean(kb.astype(jnp.float32), axis=1)).astype(jnp.bfloat16)
    kpool = jnp.concatenate([lax.optimization_barrier(jnp.max(kb, axis=1)), lax.optimization_barrier(jnp.min(kb, axis=1)), kmean], axis=-1)
    mask = block_order[None, :] > block_order[:, None]
    safe = jnp.log(jnp.where(target > 0, target, 1.0))

    def loss_of(wq, wk):
        qproj = jnp.einsum('bkgd,kde->kgbe', qpool.reshape(NB, KVH, GROUP, HD).astype(jnp.float32), wq, precision=HIGH)
        kproj = jnp.einsum('ckd,kde->kce', kpool.astype(jnp.float32), wk, precision=HIGH)
        logits = jnp.einsum('kgbe,kce->kgbc', qproj, kproj, precision=HIGH) * DG ** (-0.5)
        logits = jnp.where(mask[None, None], -1e+30, logits).reshape(QH, NB, NB)
        logp = jax.nn.log_softmax(logits, axis=-1)
        terms = jnp.where(target > 0, target * (safe - logp), 0.0)
        return jnp.sum(terms) / (QH * NB)
    loss, back = jax.vjp(loss_of, gate_query.astype(jnp.float32), gate_key.astype(jnp.float32))
    grad_query, grad_key = back(jnp.float32(1.0))
    return (loss, grad_query, grad_key)
```

```python
import functools
import math

import jax
import jax.numpy as jnp
from jax import lax
from jax.experimental import pallas as pl
from jax.experimental.pallas import tpu as pltpu
from jax.sharding import PartitionSpec as P

BLOCK = 64
MESH = pl.DeviceIdType.MESH
HIGH = lax.Precision.HIGHEST
F32 = jnp.float32
BF16 = jnp.bfloat16
MASKED = -1e30
NT = (((1,), (1,)), ((), ()))
TN = (((0,), (0,)), ((), ()))
LANES = 128
STEP = 8


def kernel(
    n, heads, group, order_ref, q_ref, k_ref, gq_ref, gk_ref,
    loss_ref, dq_ref, dk_ref,
    kbuf, bmax, bsum, ords, kmax, kmin, ksum, qpool, top, mbuf, lbuf,
    ksend, krecv, fsend, msend, mrecv, lsend, lrecv,
):
    tok, width = k_ref.shape
    rows = q_ref.shape[0]
    local = tok // BLOCK
    blocks = n * local
    span = BLOCK * group
    pair = 2 if n % 2 == 0 else 1
    far = n // pair
    scale = width ** (-0.5)
    k2 = scale * math.log2(math.e)
    me = lax.axis_index("seq")
    head = lax.axis_index("head")
    a, r = me // pair, me % pair
    partner = a * pair + (r + 1) % pair

    barrier = pltpu.get_barrier_semaphore()
    for k in range(1, n):
        pl.semaphore_signal(barrier, inc=1, device_id={"seq": (me + k) % n}, device_id_type=MESH)
    for k in range(1, heads):
        pl.semaphore_signal(barrier, inc=1, device_id={"head": (head + k) % heads}, device_id_type=MESH)

    kbuf[me, pl.ds(0, tok), :] = k_ref[...]
    row = lax.broadcasted_iota(jnp.int32, (16, width), 0)
    tail = jnp.zeros((16, width), F32)
    for i in range(local):
        tail = jnp.where(row == i, order_ref[i].astype(F32), tail)
    kbuf[me, pl.ds(tok, 16), :] = tail.astype(BF16)
    pl.semaphore_wait(barrier, n - 1 + heads - 1)

    def key_copy(slot, send, to):
        return pltpu.make_async_remote_copy(
            src_ref=kbuf.at[slot], dst_ref=kbuf.at[slot], send_sem=send, recv_sem=krecv.at[slot],
            device_id={"seq": to}, device_id_type=MESH,
        )

    sends = []
    for k in range(1, far):
        to = (a + k) % far * pair + r
        sends.append(key_copy(me, ksend.at[k], to))
    if pair == 2:
        sends.insert(1, key_copy(me, ksend.at[0], partner))
    for copy in sends:
        copy.start()

    def process(slot, own):
        data = kbuf[slot, pl.ds(0, tok), :].astype(F32)
        tail = kbuf[slot, pl.ds(tok, 16), :].astype(F32)
        for i in range(local):
            part = data[i * BLOCK:(i + 1) * BLOCK].reshape(BLOCK // 8, 8, width)
            at = slot * local + i
            kmax[at] = jnp.max(part, axis=0)
            kmin[at] = jnp.min(part, axis=0)
            ksum[at] = jnp.sum(part, axis=0)
            ords[at] = jnp.broadcast_to(tail[i:i + 1], (8, width))
        half = span // 2
        if own:
            ahead = lax.broadcasted_iota(jnp.int32, (BLOCK, half), 0) - (
                lax.broadcasted_iota(jnp.int32, (BLOCK, half), 1) // group
            )

        def columns(b, _):
            for part in range(2):
                cols = pl.ds(pl.multiple_of(b * span + part * half, half), half)
                scores = lax.dot_general(
                    kbuf[slot, pl.ds(0, tok), :], q_ref[cols, :], NT, preferred_element_type=F32
                )
                for i in range(local):
                    s = scores[i * BLOCK:(i + 1) * BLOCK]
                    if own:
                        limit = jnp.where(b == i, part * (BLOCK // 2), 2 * BLOCK)
                        s = jnp.where(ahead > limit, MASKED / k2, s)
                    s = s.reshape(BLOCK // 8, 8, half)
                    high = jnp.max(s, axis=0)
                    at = slot * local + i
                    bmax[at, :, cols] = high * k2
                    bsum[at, :, cols] = jnp.sum(jnp.exp2((s - high) * k2), axis=0)
            return 0

        lax.fori_loop(0, local, columns, 0)

    def wait_keys(slot):
        key_copy(slot, ksend.at[0], partner).wait_recv()

    process(me, True)
    forwards = []
    near = [(a - k + far) % far * pair for k in range(far)]
    order = []
    for k in range(1, far):
        slot = near[k] + r
        wait_keys(slot)
        if pair == 2:
            copy = key_copy(slot, fsend.at[k], partner)
            copy.start()
            forwards.append(copy)
            beside = near[k - 1] + (r + 1) % pair
            wait_keys(beside)
            process(beside, False)
        process(slot, False)
    if pair == 2:
        beside = near[far - 1] + (r + 1) % pair
        wait_keys(beside)
        process(beside, False)

    lane = lax.broadcasted_iota(jnp.int32, (1, LANES), 1)
    tiles = span // LANES

    def pool(b, carry):
        pooled, mine = carry
        here = order_ref[b].astype(F32)
        start = b * span

        def scores_of(c, t):
            cols = pl.ds(pl.multiple_of(start + t * LANES, LANES), LANES)
            return jnp.where(ords[c] > here, MASKED, bmax[c, :, cols]), cols

        def highest(step, high):
            for j in range(STEP):
                high = tuple(
                    jnp.maximum(high[t], scores_of(step * STEP + j, t)[0]) for t in range(tiles)
                )
            return high

        high = lax.fori_loop(
            0, blocks // STEP, highest, (jnp.full((8, LANES), MASKED, F32),) * tiles
        )
        high = [jnp.max(x, axis=0, keepdims=True) for x in high]

        def add(step, total):
            for j in range(STEP):
                out = []
                for t in range(tiles):
                    s, cols = scores_of(step * STEP + j, t)
                    out.append(total[t] + jnp.exp2(s - high[t]) * bsum[step * STEP + j, :, cols])
                total = tuple(out)
            return total

        total = lax.fori_loop(0, blocks // STEP, add, (jnp.zeros((8, LANES), F32),) * tiles)
        lse = [
            high[t] + jnp.log2(jnp.sum(total[t], axis=0, keepdims=True)) for t in range(tiles)
        ]

        def tops(step, _):
            for j in range(STEP):
                c = step * STEP + j
                best = scores_of(c, 0)[0] - lse[0]
                for t in range(1, tiles):
                    best = jnp.maximum(best, scores_of(c, t)[0] - lse[t])
                top[c] = best
            return 0

        lax.fori_loop(0, blocks // STEP, tops, 0)
        best = jnp.max(top[...], axis=1)
        shift = group
        while shift < LANES:
            best = jnp.maximum(best, pltpu.roll(best, shift, 1))
            shift *= 2
        here_lanes = lane // group == b
        qsum = jnp.sum(
            q_ref[pl.ds(pl.multiple_of(start, span), span), :].astype(F32).reshape(BLOCK, group, width),
            axis=0,
        )
        qpool[pl.ds(pl.multiple_of(b * group, group), group), :] = qsum * (1.0 / BLOCK)
        return jnp.where(here_lanes, best, pooled), jnp.where(here_lanes, here, mine)

    qpool[...] = jnp.zeros_like(qpool)
    pooled, mine = lax.fori_loop(
        0, local, pool, (jnp.zeros((blocks, LANES), F32), jnp.zeros((1, LANES), F32))
    )
    valid = lane < local * group
    pooled = jnp.exp2(pooled)
    target = pooled / jnp.sum(pooled, axis=0, keepdims=True)

    kpool = jnp.concatenate(
        [
            jnp.max(kmax[...], axis=1),
            jnp.min(kmin[...], axis=1),
            jnp.sum(ksum[...], axis=1) * (1.0 / BLOCK),
        ],
        axis=1,
    ).astype(BF16)
    qp = qpool[...].astype(BF16)
    kproj = jnp.dot(kpool, gk_ref[...], preferred_element_type=F32)
    qproj = jnp.dot(qp, gq_ref[...], preferred_element_type=F32)
    gscale = gq_ref.shape[1] ** (-0.5)
    logits = lax.dot_general(kproj, qproj, NT, precision=HIGH, preferred_element_type=F32) * gscale
    logits = jnp.where(ords[:, 0, :] > mine, MASKED, logits)
    shifted = logits - jnp.max(logits, axis=0, keepdims=True)
    weight = jnp.exp(shifted)
    norm = jnp.sum(weight, axis=0, keepdims=True)
    logp = shifted - jnp.log(norm)
    count = group * heads * blocks
    safe = jnp.log(jnp.where(target > 0, target, 1.0))
    terms = jnp.where((target > 0) & valid, target * (safe - logp), 0.0) * (1.0 / count)
    rowtot = jnp.sum(target, axis=0, keepdims=True)
    dlogit = jnp.where(valid, (weight / norm * rowtot - target) * (gscale / count), 0.0)
    mbuf[me, pl.ds(0, blocks), :] = jnp.dot(
        dlogit, qp.astype(F32), precision=HIGH, preferred_element_type=F32
    )
    mbuf[me, pl.ds(blocks, 8), :] = jnp.sum(terms.reshape(blocks // 8, 8, LANES), axis=0)

    def sum_copy(slot, k, to):
        return pltpu.make_async_remote_copy(
            src_ref=mbuf.at[slot], dst_ref=mbuf.at[slot], send_sem=msend.at[k], recv_sem=mrecv.at[slot],
            device_id={"seq": to}, device_id_type=MESH,
        )

    shares = [sum_copy(me, k, (me + k) % n) for k in range(1, n)]
    for copy in shares:
        copy.start()
    for k in range(1, n):
        sum_copy((me + k) % n, k, me).wait_recv()
    total = mbuf[0]
    for slot in range(1, n):
        total = total + mbuf[slot]

    lbuf[head] = total[blocks:]

    def loss_copy(slot, k, to):
        return pltpu.make_async_remote_copy(
            src_ref=lbuf.at[slot], dst_ref=lbuf.at[slot], send_sem=lsend.at[k], recv_sem=lrecv.at[slot],
            device_id={"head": to}, device_id_type=MESH,
        )

    losses = [loss_copy(head, k, (head + k) % heads) for k in range(1, heads)]
    for copy in losses:
        copy.start()
    grad = total[:blocks]
    dq_ref[...] = lax.dot_general(grad, kproj, TN, precision=HIGH, preferred_element_type=F32)
    dkproj = jnp.dot(grad, gq_ref[...].astype(F32), precision=HIGH, preferred_element_type=F32)
    dk_ref[...] = lax.dot_general(
        kpool.astype(F32), dkproj, TN, precision=HIGH, preferred_element_type=F32
    )
    for k in range(1, heads):
        loss_copy((head + k) % heads, k, head).wait_recv()
    loss = lbuf[0]
    for slot in range(1, heads):
        loss = loss + lbuf[slot]
    loss_ref[0, 0] = jnp.sum(loss)
    for copy in sends + forwards + shares + losses:
        copy.wait_send()


def solution(mesh):
    n, heads = mesh.shape["seq"], mesh.shape["head"]

    def shards(queries, keys, block_order, gate_query, gate_key):
        tok, group, width = queries.shape
        local = tok // BLOCK
        blocks = local * n
        dim = gate_query.shape[2]
        pooled = gate_key.shape[1]
        vmem = pl.BlockSpec(memory_space=pltpu.VMEM)
        smem = pl.BlockSpec(memory_space=pltpu.SMEM)
        dma = pltpu.SemaphoreType.DMA
        block_rows = pltpu.VMEM((blocks, 8, width), F32)
        loss, grad_q, grad_k = pl.pallas_call(
            functools.partial(kernel, n, heads, group),
            out_shape=(
                jax.ShapeDtypeStruct((1, 1), F32),
                jax.ShapeDtypeStruct((width, dim), F32),
                jax.ShapeDtypeStruct((pooled, dim), F32),
            ),
            in_specs=[smem, vmem, vmem, vmem, vmem],
            out_specs=(smem, vmem, vmem),
            scratch_shapes=[
                pltpu.VMEM((n, tok + 16, width), BF16),
                pltpu.VMEM((blocks, 8, tok * group), F32),
                pltpu.VMEM((blocks, 8, tok * group), F32),
                block_rows,
                block_rows,
                block_rows,
                block_rows,
                pltpu.VMEM((LANES, width), F32),
                block_rows,
                pltpu.VMEM((n, blocks + 8, width), F32),
                pltpu.VMEM((heads, 8, width), F32),
                dma((n,)), dma((n,)), dma((n,)), dma((n,)), dma((n,)), dma((heads,)), dma((heads,)),
            ],
            compiler_params=pltpu.CompilerParams(
                collective_id=0, has_side_effects=True, vmem_limit_bytes=48 << 20
            ),
        )(
            block_order,
            queries.reshape(tok * group, width),
            keys.reshape(tok, width),
            gate_query[0],
            gate_key[0],
        )
        return loss[0, 0], grad_q[None], grad_k[None]

    return jax.shard_map(
        shards,
        mesh=mesh,
        in_specs=(
            P("seq", "head", None),
            P("seq", "head", None),
            P("seq"),
            P("head", None, None),
            P("head", None, None),
        ),
        out_specs=(P(), P("head", None, None), P("head", None, None)),
        check_vma=False,
    )
```

```python
import functools
import math

import jax
import jax.numpy as jnp
from jax import lax
from jax.experimental import pallas as pl
from jax.experimental.pallas import tpu as pltpu
from jax.sharding import PartitionSpec as P

BLOCK = 64
MESH = pl.DeviceIdType.MESH
HIGH = lax.Precision.HIGHEST
F32 = jnp.float32
BF16 = jnp.bfloat16
MASKED = -1e30
NT = (((1,), (1,)), ((), ()))
TN = (((0,), (0,)), ((), ()))
LANES = 128
STEP = 32


def kernel(
    n, heads, group, order_hbm, q_hbm, k_hbm, gq_hbm, gk_hbm,
    loss_ref, dq_ref, dk_ref,
    kbuf, bmax, rmax, rsum, ords, kmax, kmin, ksum, top, mbuf, lbuf,
    order_ref, q_ref, qt, gq_ref, gk_ref,
    ksend, krecv, fsend, msend, mrecv, lsend, lrecv, held,
):
    tok, width = k_hbm.shape
    local = tok // BLOCK
    blocks = n * local
    span = BLOCK * group
    pair = 2 if n % 2 == 0 else 1
    far = n // pair
    scale = width ** (-0.5)
    k2 = scale * math.log2(math.e)
    me = lax.axis_index("seq")
    head = lax.axis_index("head")
    a, r = me // pair, me % pair
    partner = a * pair + (r + 1) % pair

    barrier = pltpu.get_barrier_semaphore()
    for k in range(1, n):
        pl.semaphore_signal(barrier, inc=1, device_id={"seq": (me + k) % n}, device_id_type=MESH)
    for k in range(1, heads):
        pl.semaphore_signal(barrier, inc=1, device_id={"head": (head + k) % heads}, device_id_type=MESH)

    fetch = [
        pltpu.make_async_copy(k_hbm, kbuf.at[me, pl.ds(0, tok), :], held.at[0]),
        pltpu.make_async_copy(order_hbm, order_ref, held.at[1]),
        pltpu.make_async_copy(q_hbm, q_ref, held.at[2]),
        pltpu.make_async_copy(gq_hbm, gq_ref, held.at[3]),
        pltpu.make_async_copy(gk_hbm, gk_ref, held.at[4]),
    ]
    for copy in fetch:
        copy.start()

    fetch[1].wait()
    row = lax.broadcasted_iota(jnp.int32, (16, width), 0)
    tail = jnp.zeros((16, width), F32)
    for i in range(local):
        tail = jnp.where(row == i, order_ref[i].astype(F32), tail)
    kbuf[me, pl.ds(tok, 16), :] = tail.astype(BF16)
    fetch[0].wait()
    pl.semaphore_wait(barrier, n - 1 + heads - 1)

    def key_copy(slot, send, to):
        return pltpu.make_async_remote_copy(
            src_ref=kbuf.at[slot], dst_ref=kbuf.at[slot], send_sem=send, recv_sem=krecv.at[slot],
            device_id={"seq": to}, device_id_type=MESH,
        )

    sends = []
    for k in range(1, far):
        to = (a + k) % far * pair + r
        sends.append(key_copy(me, ksend.at[k], to))
    if pair == 2:
        sends.insert(1, key_copy(me, ksend.at[0], partner))
    for copy in sends:
        copy.start()

    fetch[2].wait()
    qpool = []
    for b in range(local):
        data = q_ref[pl.ds(b * span, span), :]
        qt[:, pl.ds(b * span, span)] = data.T
        qpool.append(jnp.sum(data.astype(F32).reshape(BLOCK, group, width), axis=0))
    qpool.append(jnp.zeros((LANES - local * group, width), F32))
    qp = (jnp.concatenate(qpool, axis=0) * (1.0 / BLOCK)).astype(BF16)
    fetch[3].wait()
    fetch[4].wait()
    qproj = jnp.dot(qp, gq_ref[...], preferred_element_type=F32)
    rmax[...] = jnp.full_like(rmax, MASKED)
    rsum[...] = jnp.zeros_like(rsum)

    half = span // 2

    def process(slot, own):
        data = kbuf[slot, pl.ds(0, tok), :].astype(F32)
        tail = kbuf[slot, pl.ds(tok, 16), :].astype(F32)
        for i in range(local):
            part = data[i * BLOCK:(i + 1) * BLOCK].reshape(BLOCK // 8, 8, width)
            at = slot * local + i
            kmax[at] = jnp.max(part, axis=0)
            kmin[at] = jnp.min(part, axis=0)
            ksum[at] = jnp.sum(part, axis=0)
            ords[at] = jnp.broadcast_to(tail[i:i + 1], (8, width))
        if own:
            ahead = lax.broadcasted_iota(jnp.int32, (BLOCK, half), 0) - (
                lax.broadcasted_iota(jnp.int32, (BLOCK, half), 1) // group
            )

        def tile(b, part):
            cols = pl.ds(pl.multiple_of(b * span + part * half, half), half)
            here = order_ref[b].astype(F32)
            scores = jnp.dot(
                kbuf[slot, pl.ds(0, tok), :], qt[:, cols], preferred_element_type=F32
            )
            highs, sums = [], []
            for i in range(local):
                s = scores[i * BLOCK:(i + 1) * BLOCK]
                if own:
                    limit = jnp.where(b == i, part * (BLOCK // 2), 2 * BLOCK)
                    s = jnp.where(ahead > limit, MASKED / k2, s)
                s = s.reshape(BLOCK // 8, 8, half)
                high = jnp.max(s, axis=0)
                sums.append(jnp.sum(jnp.exp2((s - high) * k2), axis=0))
                later = jnp.broadcast_to(tail[i:i + 1, :1], (8, half)) > here
                high = jnp.where(later, MASKED, high * k2)
                bmax[slot * local + i, :, cols] = high
                highs.append(high)
            old = rmax[:, cols]
            new = functools.reduce(jnp.maximum, highs, old)
            total = rsum[:, cols] * jnp.exp2(old - new)
            for high, amount in zip(highs, sums):
                total = total + amount * jnp.exp2(high - new)
            rmax[:, cols] = new
            rsum[:, cols] = total

        def columns(step, _):
            for b in range(2):
                for part in range(2):
                    tile(step * 2 + b, part)
            return 0

        lax.fori_loop(0, local // 2, columns, 0)

    def wait_keys(slot):
        key_copy(slot, ksend.at[0], partner).wait_recv()

    process(me, True)
    forwards = []
    near = [(a - k + far) % far * pair for k in range(far)]
    for k in range(1, far):
        slot = near[k] + r
        wait_keys(slot)
        if pair == 2:
            copy = key_copy(slot, fsend.at[k], partner)
            copy.start()
            forwards.append(copy)
            beside = near[k - 1] + (r + 1) % pair
            wait_keys(beside)
            process(beside, False)
        process(slot, False)
    if pair == 2:
        beside = near[far - 1] + (r + 1) % pair
        wait_keys(beside)
        process(beside, False)

    kpool = jnp.concatenate(
        [
            jnp.max(kmax[...], axis=1),
            jnp.min(kmin[...], axis=1),
            jnp.sum(ksum[...], axis=1) * (1.0 / BLOCK),
        ],
        axis=1,
    ).astype(BF16)
    kproj = jnp.dot(kpool, gk_ref[...], preferred_element_type=F32)

    lane = lax.broadcasted_iota(jnp.int32, (1, LANES), 1)
    tiles = span // LANES
    pooled = jnp.zeros((blocks, LANES), F32)
    mine = jnp.zeros((1, LANES), F32)
    for b in range(local):
        lse = []
        for t in range(tiles):
            cols = pl.ds(b * span + t * LANES, LANES)
            part = rmax[:, cols]
            high = jnp.max(part, axis=0, keepdims=True)
            total = jnp.sum(rsum[:, cols] * jnp.exp2(part - high), axis=0, keepdims=True)
            lse.append(high + jnp.log2(total))

        def tops(step, _):
            for j in range(STEP):
                c = step * STEP + j
                best = [
                    bmax[c, :, pl.ds(b * span + t * LANES, LANES)] - lse[t] for t in range(tiles)
                ]
                top[b, c] = functools.reduce(jnp.maximum, best)
            return 0

        lax.fori_loop(0, blocks // STEP, tops, 0)
        best = jnp.max(top[b], axis=1)
        shift = group
        while shift < LANES:
            best = jnp.maximum(best, pltpu.roll(best, shift, 1))
            shift *= 2
        here_lanes = lane // group == b
        pooled = jnp.where(here_lanes, best, pooled)
        mine = jnp.where(here_lanes, order_ref[b].astype(F32), mine)
    valid = lane < local * group
    pooled = jnp.exp2(pooled)
    target = pooled / jnp.sum(pooled, axis=0, keepdims=True)

    gscale = gq_ref.shape[1] ** (-0.5)
    logits = lax.dot_general(kproj, qproj, NT, precision=HIGH, preferred_element_type=F32) * gscale
    logits = jnp.where(ords[:, 0, :] > mine, MASKED, logits)
    shifted = logits - jnp.max(logits, axis=0, keepdims=True)
    weight = jnp.exp(shifted)
    norm = jnp.sum(weight, axis=0, keepdims=True)
    logp = shifted - jnp.log(norm)
    count = group * heads * blocks
    safe = jnp.log(jnp.where(target > 0, target, 1.0))
    terms = jnp.where((target > 0) & valid, target * (safe - logp), 0.0) * (1.0 / count)
    rowtot = jnp.sum(target, axis=0, keepdims=True)
    dlogit = jnp.where(valid, (weight / norm * rowtot - target) * (gscale / count), 0.0)
    mbuf[me, pl.ds(0, blocks), :] = jnp.dot(
        dlogit, qp.astype(F32), precision=HIGH, preferred_element_type=F32
    )
    mbuf[me, pl.ds(blocks, 8), :] = jnp.sum(terms.reshape(blocks // 8, 8, LANES), axis=0)

    def sum_copy(slot, k, to):
        return pltpu.make_async_remote_copy(
            src_ref=mbuf.at[slot], dst_ref=mbuf.at[slot], send_sem=msend.at[k], recv_sem=mrecv.at[slot],
            device_id={"seq": to}, device_id_type=MESH,
        )

    shares = [sum_copy(me, k, (me + k) % n) for k in range(1, n)]
    for copy in shares:
        copy.start()
    for k in range(1, n):
        sum_copy((me + k) % n, k, me).wait_recv()
    total = mbuf[0]
    for slot in range(1, n):
        total = total + mbuf[slot]

    lbuf[head] = total[blocks:]

    def loss_copy(slot, k, to):
        return pltpu.make_async_remote_copy(
            src_ref=lbuf.at[slot], dst_ref=lbuf.at[slot], send_sem=lsend.at[k], recv_sem=lrecv.at[slot],
            device_id={"head": to}, device_id_type=MESH,
        )

    losses = [loss_copy(head, k, (head + k) % heads) for k in range(1, heads)]
    for copy in losses:
        copy.start()
    grad = total[:blocks]
    dq_ref[...] = lax.dot_general(grad, kproj, TN, precision=HIGH, preferred_element_type=F32)
    dkproj = jnp.dot(grad, gq_ref[...].astype(F32), precision=HIGH, preferred_element_type=F32)
    dk_ref[...] = lax.dot_general(
        kpool.astype(F32), dkproj, TN, precision=HIGH, preferred_element_type=F32
    )
    for k in range(1, heads):
        loss_copy((head + k) % heads, k, head).wait_recv()
    loss = lbuf[0]
    for slot in range(1, heads):
        loss = loss + lbuf[slot]
    loss_ref[0, 0] = jnp.sum(loss)
    for copy in sends + forwards + shares + losses:
        copy.wait_send()


def solution(mesh):
    n, heads = mesh.shape["seq"], mesh.shape["head"]

    def shards(queries, keys, block_order, gate_query, gate_key):
        tok, group, width = queries.shape
        local = tok // BLOCK
        blocks = local * n
        dim = gate_query.shape[2]
        pooled = gate_key.shape[1]
        vmem = pl.BlockSpec(memory_space=pltpu.VMEM)
        hbm = pl.BlockSpec(memory_space=pltpu.HBM)
        smem = pl.BlockSpec(memory_space=pltpu.SMEM)
        dma = pltpu.SemaphoreType.DMA
        block_rows = pltpu.VMEM((blocks, 8, width), F32)
        loss, grad_q, grad_k = pl.pallas_call(
            functools.partial(kernel, n, heads, group),
            out_shape=(
                jax.ShapeDtypeStruct((1, 1), F32),
                jax.ShapeDtypeStruct((width, dim), F32),
                jax.ShapeDtypeStruct((pooled, dim), F32),
            ),
            in_specs=[hbm] * 5,
            out_specs=(smem, vmem, vmem),
            scratch_shapes=[
                pltpu.VMEM((n, tok + 16, width), BF16),
                pltpu.VMEM((blocks, 8, tok * group), F32),
                pltpu.VMEM((8, tok * group), F32),
                pltpu.VMEM((8, tok * group), F32),
                block_rows,
                block_rows,
                block_rows,
                block_rows,
                pltpu.VMEM((local, blocks, 8, width), F32),
                pltpu.VMEM((n, blocks + 8, width), F32),
                pltpu.VMEM((heads, 8, width), F32),
                pltpu.SMEM((local,), jnp.int32),
                pltpu.VMEM((tok * group, width), BF16),
                pltpu.VMEM((width, tok * group), BF16),
                pltpu.VMEM((width, dim), BF16),
                pltpu.VMEM((pooled, dim), BF16),
                dma((n,)), dma((n,)), dma((n,)), dma((n,)), dma((n,)), dma((heads,)), dma((heads,)), dma((5,)),
            ],
            compiler_params=pltpu.CompilerParams(
                collective_id=0, has_side_effects=True, vmem_limit_bytes=64 << 20
            ),
        )(
            block_order,
            queries.reshape(tok * group, width),
            keys.reshape(tok, width),
            gate_query[0],
            gate_key[0],
        )
        return loss[0, 0], grad_q[None], grad_k[None]

    return jax.shard_map(
        shards,
        mesh=mesh,
        in_specs=(
            P("seq", "head", None),
            P("seq", "head", None),
            P("seq"),
            P("head", None, None),
            P("head", None, None),
        ),
        out_specs=(P(), P("head", None, None), P("head", None, None)),
        check_vma=False,
    )
```

```python
import functools
import math

import jax
import jax.numpy as jnp
from jax import lax
from jax.experimental import pallas as pl
from jax.experimental.pallas import tpu as pltpu
from jax.sharding import PartitionSpec as P

BLOCK = 64
MESH = pl.DeviceIdType.MESH
HIGH = lax.Precision.HIGHEST
F32 = jnp.float32
BF16 = jnp.bfloat16
MASKED = -1e30
NT = (((1,), (1,)), ((), ()))
TN = (((0,), (0,)), ((), ()))
LANES = 128
STEP = 32


def kernel(
    n, heads, group, order_hbm, q_hbm, k_hbm, gq_hbm, gk_hbm,
    loss_ref, dq_ref, dk_ref,
    kbuf, bmax, rmax, rsum, ords, kmax, kmin, kmean, top, mbuf, lbuf,
    order_ref, q_ref, qt, gq_ref, gk_ref,
    ksend, krecv, fsend, msend, mrecv, lsend, lrecv, held,
):
    tok, width = k_hbm.shape
    local = tok // BLOCK
    extra = kbuf.shape[1] - tok
    blocks = n * local
    span = BLOCK * group
    far = n // 2
    scale = width ** (-0.5)
    k2 = scale * math.log2(math.e)
    me = lax.axis_index("seq")
    head = lax.axis_index("head")
    a, r = me // 2, me % 2
    partner = a * 2 + (r + 1) % 2

    barrier = pltpu.get_barrier_semaphore()
    for k in range(1, n):
        pl.semaphore_signal(barrier, inc=1, device_id={"seq": (me + k) % n}, device_id_type=MESH)
    for k in range(1, heads):
        pl.semaphore_signal(barrier, inc=1, device_id={"head": (head + k) % heads}, device_id_type=MESH)

    fetch = [
        pltpu.make_async_copy(k_hbm, kbuf.at[me, pl.ds(0, tok), :], held.at[0]),
        pltpu.make_async_copy(order_hbm, order_ref, held.at[1]),
        pltpu.make_async_copy(q_hbm, q_ref, held.at[2]),
        pltpu.make_async_copy(gq_hbm, gq_ref, held.at[3]),
        pltpu.make_async_copy(gk_hbm, gk_ref, held.at[4]),
    ]
    for copy in fetch:
        copy.start()

    fetch[1].wait()
    fetch[0].wait()
    row = lax.broadcasted_iota(jnp.int32, (extra, width), 0)
    tail = jnp.zeros((extra, width), F32)
    for i in range(local):
        part = kbuf[me, pl.ds(i * BLOCK, BLOCK), :].astype(F32).reshape(BLOCK // 8, 8, width)
        pieces = (
            order_ref[i].astype(F32),
            jnp.max(jnp.max(part, axis=0), axis=0, keepdims=True),
            jnp.min(jnp.min(part, axis=0), axis=0, keepdims=True),
            jnp.sum(jnp.sum(part, axis=0), axis=0, keepdims=True) * (1.0 / BLOCK),
        )
        for m, piece in enumerate(pieces):
            tail = jnp.where(row == 4 * i + m, piece, tail)
    kbuf[me, pl.ds(tok, extra), :] = tail.astype(BF16)
    pl.semaphore_wait(barrier, n - 1 + heads - 1)

    def key_copy(slot, send, to):
        return pltpu.make_async_remote_copy(
            src_ref=kbuf.at[slot], dst_ref=kbuf.at[slot], send_sem=send, recv_sem=krecv.at[slot],
            device_id={"seq": to}, device_id_type=MESH,
        )

    sends = []
    for k in range(1, far):
        to = (a + k) % far * 2 + r
        sends.append(key_copy(me, ksend.at[k], to))
    sends.insert(1, key_copy(me, ksend.at[0], partner))
    for copy in sends:
        copy.start()

    fetch[2].wait()
    qpool = []
    for b in range(local):
        data = q_ref[pl.ds(b * span, span), :]
        qt[:, pl.ds(b * span, span)] = data.T
        qpool.append(jnp.sum(data.astype(F32).reshape(BLOCK, group, width), axis=0))
    qpool.append(jnp.zeros((LANES - local * group, width), F32))
    qp = (jnp.concatenate(qpool, axis=0) * (1.0 / BLOCK)).astype(BF16)
    fetch[3].wait()
    fetch[4].wait()
    qproj = jnp.dot(qp, gq_ref[...], preferred_element_type=F32)
    rmax[...] = jnp.full_like(rmax, MASKED)
    rsum[...] = jnp.zeros_like(rsum)

    half = span // 2

    ahead = lax.broadcasted_iota(jnp.int32, (BLOCK, half), 0) - (
        lax.broadcasted_iota(jnp.int32, (BLOCK, half), 1) // group
    )

    def wait_keys(slot):
        key_copy(slot, ksend.at[0], partner).wait_recv()

    def shard(j, _):
        back = j // 2
        slot = (a - back + far) % far * 2 + (r + j) % 2

        @pl.when((j % 2 == 1) & (back + 1 < far))
        def _():
            direct = (a - back - 1 + far) % far * 2 + r
            wait_keys(direct)
            key_copy(direct, fsend.at[back + 1], partner).start()

        @pl.when(j % 2 == 1)
        def _():
            wait_keys(slot)

        tail = kbuf[slot, pl.ds(tok, extra), :].astype(F32)
        for i in range(local):
            at = slot * local + i
            for m, ref in enumerate((ords, kmax, kmin, kmean)):
                ref[at] = jnp.broadcast_to(tail[4 * i + m:4 * i + m + 1], (8, width))
        unmasked = jnp.where(j == 0, 0, 2 * BLOCK)

        for b in range(local):
            here = order_ref[b].astype(F32)
            for part in range(2):
                cols = pl.ds(b * span + part * half, half)
                scores = jnp.dot(
                    kbuf[slot, pl.ds(0, tok), :], qt[:, cols], preferred_element_type=F32
                )
                highs, sums = [], []
                for i in range(local):
                    s = scores[i * BLOCK:(i + 1) * BLOCK]
                    if b == i:
                        s = jnp.where(ahead > unmasked + part * (BLOCK // 2), MASKED / k2, s)
                    s = s.reshape(BLOCK // 8, 8, half)
                    high = jnp.max(s, axis=0)
                    sums.append(jnp.sum(jnp.exp2((s - high) * k2), axis=0))
                    later = jnp.broadcast_to(tail[4 * i:4 * i + 1, :1], (8, half)) > here
                    high = jnp.where(later, MASKED, high * k2)
                    bmax[slot * local + i, :, cols] = high
                    highs.append(high)
                old = rmax[:, cols]
                new = functools.reduce(jnp.maximum, highs, old)
                total = rsum[:, cols] * jnp.exp2(old - new)
                for high, amount in zip(highs, sums):
                    total = total + amount * jnp.exp2(high - new)
                rmax[:, cols] = new
                rsum[:, cols] = total
        return 0

    lax.fori_loop(0, n, shard, 0)
    forwards = [
        key_copy((a - k + far) % far * 2 + r, fsend.at[k], partner) for k in range(1, far)
    ]

    kpool = jnp.concatenate([ref[:, 0, :] for ref in (kmax, kmin, kmean)], axis=1).astype(BF16)
    kproj = jnp.dot(kpool, gk_ref[...], preferred_element_type=F32)

    lane = lax.broadcasted_iota(jnp.int32, (1, LANES), 1)
    tiles = span // LANES
    pooled = jnp.zeros((blocks, LANES), F32)
    mine = jnp.zeros((1, LANES), F32)
    for b in range(local):
        lse = []
        for t in range(tiles):
            cols = pl.ds(b * span + t * LANES, LANES)
            part = rmax[:, cols]
            high = jnp.max(part, axis=0, keepdims=True)
            total = jnp.sum(rsum[:, cols] * jnp.exp2(part - high), axis=0, keepdims=True)
            lse.append(high + jnp.log2(total))

        def tops(step, _):
            for j in range(STEP):
                c = step * STEP + j
                best = [
                    bmax[c, :, pl.ds(b * span + t * LANES, LANES)] - lse[t] for t in range(tiles)
                ]
                top[b, c] = functools.reduce(jnp.maximum, best)
            return 0

        lax.fori_loop(0, blocks // STEP, tops, 0)
        best = jnp.max(top[b], axis=1)
        shift = group
        while shift < LANES:
            best = jnp.maximum(best, pltpu.roll(best, shift, 1))
            shift *= 2
        here_lanes = lane // group == b
        pooled = jnp.where(here_lanes, best, pooled)
        mine = jnp.where(here_lanes, order_ref[b].astype(F32), mine)
    valid = lane < local * group
    pooled = jnp.exp2(pooled)
    target = pooled / jnp.sum(pooled, axis=0, keepdims=True)

    gscale = gq_ref.shape[1] ** (-0.5)
    logits = lax.dot_general(kproj, qproj, NT, precision=HIGH, preferred_element_type=F32) * gscale
    logits = jnp.where(ords[:, 0, :] > mine, MASKED, logits)
    shifted = logits - jnp.max(logits, axis=0, keepdims=True)
    weight = jnp.exp(shifted)
    norm = jnp.sum(weight, axis=0, keepdims=True)
    logp = shifted - jnp.log(norm)
    count = group * heads * blocks
    safe = jnp.log(jnp.where(target > 0, target, 1.0))
    terms = jnp.where((target > 0) & valid, target * (safe - logp), 0.0) * (1.0 / count)
    rowtot = jnp.sum(target, axis=0, keepdims=True)
    dlogit = jnp.where(valid, (weight / norm * rowtot - target) * (gscale / count), 0.0)
    mbuf[me, pl.ds(0, blocks), :] = jnp.dot(
        dlogit, qp.astype(F32), precision=HIGH, preferred_element_type=F32
    )
    mbuf[me, pl.ds(blocks, 8), :] = jnp.sum(terms.reshape(blocks // 8, 8, LANES), axis=0)

    def sum_copy(slot, k, to):
        return pltpu.make_async_remote_copy(
            src_ref=mbuf.at[slot], dst_ref=mbuf.at[slot], send_sem=msend.at[k], recv_sem=mrecv.at[slot],
            device_id={"seq": to}, device_id_type=MESH,
        )

    shares = [sum_copy(me, k, (me + k) % n) for k in range(1, n)]
    for copy in shares:
        copy.start()
    for k in range(1, n):
        sum_copy((me + k) % n, k, me).wait_recv()
    total = mbuf[0]
    for slot in range(1, n):
        total = total + mbuf[slot]

    lbuf[head] = total[blocks:]

    def loss_copy(slot, k, to):
        return pltpu.make_async_remote_copy(
            src_ref=lbuf.at[slot], dst_ref=lbuf.at[slot], send_sem=lsend.at[k], recv_sem=lrecv.at[slot],
            device_id={"head": to}, device_id_type=MESH,
        )

    losses = [loss_copy(head, k, (head + k) % heads) for k in range(1, heads)]
    for copy in losses:
        copy.start()
    grad = total[:blocks]
    dq_ref[...] = lax.dot_general(grad, kproj, TN, precision=HIGH, preferred_element_type=F32)
    dkproj = jnp.dot(grad, gq_ref[...].astype(F32), precision=HIGH, preferred_element_type=F32)
    dk_ref[...] = lax.dot_general(
        kpool.astype(F32), dkproj, TN, precision=HIGH, preferred_element_type=F32
    )
    for k in range(1, heads):
        loss_copy((head + k) % heads, k, head).wait_recv()
    loss = lbuf[0]
    for slot in range(1, heads):
        loss = loss + lbuf[slot]
    loss_ref[0, 0] = jnp.sum(loss)
    for copy in sends + forwards + shares + losses:
        copy.wait_send()


def solution(mesh):
    n, heads = mesh.shape["seq"], mesh.shape["head"]

    def shards(queries, keys, block_order, gate_query, gate_key):
        tok, group, width = queries.shape
        local = tok // BLOCK
        blocks = local * n
        extra = -(-4 * local // 16) * 16
        dim = gate_query.shape[2]
        pooled = gate_key.shape[1]
        vmem = pl.BlockSpec(memory_space=pltpu.VMEM)
        hbm = pl.BlockSpec(memory_space=pltpu.HBM)
        smem = pl.BlockSpec(memory_space=pltpu.SMEM)
        dma = pltpu.SemaphoreType.DMA
        block_rows = pltpu.VMEM((blocks, 8, width), F32)
        loss, grad_q, grad_k = pl.pallas_call(
            functools.partial(kernel, n, heads, group),
            out_shape=(
                jax.ShapeDtypeStruct((1, 1), F32),
                pltpu.VMEM((width, dim), F32),
                pltpu.VMEM((pooled, dim), F32),
            ),
            in_specs=[hbm] * 5,
            out_specs=(smem, vmem, vmem),
            scratch_shapes=[
                pltpu.VMEM((n, tok + extra, width), BF16),
                pltpu.VMEM((blocks, 8, tok * group), F32),
                pltpu.VMEM((8, tok * group), F32),
                pltpu.VMEM((8, tok * group), F32),
                block_rows,
                block_rows,
                block_rows,
                block_rows,
                pltpu.VMEM((local, blocks, 8, width), F32),
                pltpu.VMEM((n, blocks + 8, width), F32),
                pltpu.VMEM((heads, 8, width), F32),
                pltpu.SMEM((local,), jnp.int32),
                pltpu.VMEM((tok * group, width), BF16),
                pltpu.VMEM((width, tok * group), BF16),
                pltpu.VMEM((width, dim), BF16),
                pltpu.VMEM((pooled, dim), BF16),
                dma((n,)), dma((n,)), dma((n,)), dma((n,)), dma((n,)), dma((heads,)), dma((heads,)), dma((5,)),
            ],
            compiler_params=pltpu.CompilerParams(
                collective_id=0, has_side_effects=True, vmem_limit_bytes=48 << 20
            ),
        )(
            *(
                pltpu.with_memory_space_constraint(x, pltpu.HBM)
                for x in (
                    block_order,
                    queries.reshape(tok * group, width),
                    keys.reshape(tok, width),
                    gate_query[0],
                    gate_key[0],
                )
            )
        )
        return loss[0, 0], grad_q[None], grad_k[None]

    return jax.shard_map(
        shards,
        mesh=mesh,
        in_specs=(
            P("seq", "head", None),
            P("seq", "head", None),
            P("seq"),
            P("head", None, None),
            P("head", None, None),
        ),
        out_specs=(P(), P("head", None, None), P("head", None, None)),
        check_vma=False,
    )
```

```python
import functools
import math

import jax
import jax.numpy as jnp
from jax import lax
from jax.experimental import pallas as pl
from jax.experimental.pallas import tpu as pltpu
from jax.sharding import PartitionSpec as P

BLOCK = 64
MESH = pl.DeviceIdType.MESH
F32 = jnp.float32
BF16 = jnp.bfloat16
MASKED = -1e30
NT = (((1,), (1,)), ((), ()))
TN = (((0,), (0,)), ((), ()))
LANES = 128
STEP = 32


def parts(x):
    high = x.astype(BF16)
    return high, (x - high.astype(F32)).astype(BF16)


def product(x, y, dims=(((1,), (0,)), ((), ()))):
    (xc,), (yc,) = dims[0]
    xs = parts(x) if x.dtype == F32 else (x,)
    ys = parts(y) if y.dtype == F32 else (y,)
    pairs = [(i, j) for i in range(len(xs)) for j in range(len(ys)) if i + j < 2]
    left = jnp.concatenate([xs[i] for i, _ in pairs], axis=xc)
    right = jnp.concatenate([ys[j] for _, j in pairs], axis=yc)
    return lax.dot_general(left, right, dims, preferred_element_type=F32)


def kernel(
    n, heads, group, order_hbm, q_hbm, k_hbm, gq_hbm, gk_hbm,
    loss_ref, dq_ref, dk_ref,
    kbuf, bmax, rmax, rsum, ords, kmax, kmin, kmean, top, mbuf, lbuf,
    order_ref, q_ref, qt, gq_ref, gk_ref,
    ksend, krecv, fsend, msend, mrecv, lsend, lrecv, held,
):
    tok, width = k_hbm.shape
    local = tok // BLOCK
    width_q = local * group
    extra = kbuf.shape[1] - tok - width_q
    blocks = n * local
    span = BLOCK * group
    far = n // 2
    k2 = width ** (-0.5) * math.log2(math.e)
    me = lax.axis_index("seq")
    head = lax.axis_index("head")
    a, r = me // 2, me % 2
    partner = a * 2 + (r + 1) % 2

    barrier = pltpu.get_barrier_semaphore()
    for k in range(1, n):
        pl.semaphore_signal(barrier, inc=1, device_id={"seq": (me + k) % n}, device_id_type=MESH)
    for k in range(1, heads):
        pl.semaphore_signal(barrier, inc=1, device_id={"head": (head + k) % heads}, device_id_type=MESH)

    fetch = [
        pltpu.make_async_copy(k_hbm, kbuf.at[me, pl.ds(0, tok), :], held.at[0]),
        pltpu.make_async_copy(order_hbm, order_ref, held.at[1]),
        pltpu.make_async_copy(q_hbm, q_ref, held.at[2]),
        pltpu.make_async_copy(gq_hbm, gq_ref, held.at[3]),
        pltpu.make_async_copy(gk_hbm, gk_ref, held.at[4]),
    ]
    for copy in fetch:
        copy.start()

    fetch[1].wait()
    fetch[0].wait()
    row = lax.broadcasted_iota(jnp.int32, (extra, width), 0)
    tail = jnp.zeros((extra, width), F32)
    for i in range(local):
        part = kbuf[me, pl.ds(i * BLOCK, BLOCK), :].astype(F32).reshape(BLOCK // 8, 8, width)
        pieces = (
            order_ref[i].astype(F32),
            jnp.max(jnp.max(part, axis=0), axis=0, keepdims=True),
            jnp.min(jnp.min(part, axis=0), axis=0, keepdims=True),
            jnp.sum(jnp.sum(part, axis=0), axis=0, keepdims=True) * (1.0 / BLOCK),
        )
        for m, piece in enumerate(pieces):
            tail = jnp.where(row == 4 * i + m, piece, tail)
    kbuf[me, pl.ds(tok, extra), :] = tail.astype(BF16)
    fetch[2].wait()
    qpool = [
        jnp.sum(
            q_ref[pl.ds(b * span, span), :].astype(F32).reshape(BLOCK, group, width), axis=0
        )
        for b in range(local)
    ]
    qp = (jnp.concatenate(qpool, axis=0) * (1.0 / BLOCK)).astype(BF16)
    kbuf[me, pl.ds(tok + extra, width_q), :] = qp
    pl.semaphore_wait(barrier, n - 1 + heads - 1)

    def key_copy(slot, send, to):
        return pltpu.make_async_remote_copy(
            src_ref=kbuf.at[slot], dst_ref=kbuf.at[slot], send_sem=send, recv_sem=krecv.at[slot],
            device_id={"seq": to}, device_id_type=MESH,
        )

    sends = []
    for k in range(1, far):
        to = (a + k) % far * 2 + r
        sends.append(key_copy(me, ksend.at[k], to))
    sends.insert(1, key_copy(me, ksend.at[0], partner))
    for copy in sends:
        copy.start()

    for b in range(local):
        qt[:, pl.ds(b * span, span)] = q_ref[pl.ds(b * span, span), :].T
    fetch[3].wait()
    fetch[4].wait()
    qproj = jnp.dot(qp, gq_ref[...], preferred_element_type=F32)
    qproj = jnp.concatenate([qproj, jnp.zeros((LANES - width_q, qproj.shape[1]), F32)], axis=0)
    rmax[...] = jnp.full_like(rmax, MASKED)
    rsum[...] = jnp.zeros_like(rsum)

    half = span // 2

    ahead = lax.broadcasted_iota(jnp.int32, (BLOCK, half), 0) - (
        lax.broadcasted_iota(jnp.int32, (BLOCK, half), 1) // group
    )

    def wait_keys(slot):
        key_copy(slot, ksend.at[0], partner).wait_recv()

    def shard(j, _):
        back = j // 2
        slot = (a - back + far) % far * 2 + (r + j) % 2

        @pl.when((j % 2 == 1) & (back + 1 < far))
        def _():
            direct = (a - back - 1 + far) % far * 2 + r
            wait_keys(direct)
            key_copy(direct, fsend.at[back + 1], partner).start()

        @pl.when(j % 2 == 1)
        def _():
            wait_keys(slot)

        tail = kbuf[slot, pl.ds(tok, extra), :].astype(F32)
        for i in range(local):
            at = slot * local + i
            for m, ref in enumerate((ords, kmax, kmin, kmean)):
                ref[at] = jnp.broadcast_to(tail[4 * i + m:4 * i + m + 1], (8, width))
        unmasked = jnp.where(j == 0, 0, 2 * BLOCK)

        for b in range(local):
            here = order_ref[b].astype(F32)
            for part in range(2):
                cols = pl.ds(b * span + part * half, half)
                scores = jnp.dot(
                    kbuf[slot, pl.ds(0, tok), :], qt[:, cols], preferred_element_type=F32
                )
                highs, sums = [], []
                for i in range(local):
                    s = scores[i * BLOCK:(i + 1) * BLOCK]
                    if b == i:
                        s = jnp.where(ahead > unmasked + part * (BLOCK // 2), MASKED / k2, s)
                    s = s.reshape(BLOCK // 8, 8, half)
                    high = jnp.max(s, axis=0)
                    sums.append(jnp.sum(jnp.exp2((s - high) * k2), axis=0))
                    later = jnp.broadcast_to(tail[4 * i:4 * i + 1, :1], (8, half)) > here
                    high = jnp.where(later, MASKED, high * k2)
                    bmax[slot * local + i, :, cols] = high
                    highs.append(high)
                old = rmax[:, cols]
                new = functools.reduce(jnp.maximum, highs, old)
                total = rsum[:, cols] * jnp.exp2(old - new)
                for high, amount in zip(highs, sums):
                    total = total + amount * jnp.exp2(high - new)
                rmax[:, cols] = new
                rsum[:, cols] = total
        return 0

    lax.fori_loop(0, n, shard, 0)
    forwards = [
        key_copy((a - k + far) % far * 2 + r, fsend.at[k], partner) for k in range(1, far)
    ]

    kpool = jnp.concatenate([ref[:, 0, :] for ref in (kmax, kmin, kmean)], axis=1).astype(BF16)
    kproj = jnp.dot(kpool, gk_ref[...], preferred_element_type=F32)

    lane = lax.broadcasted_iota(jnp.int32, (1, LANES), 1)
    tiles = span // LANES
    pooled = jnp.zeros((blocks, LANES), F32)
    mine = jnp.zeros((1, LANES), F32)
    for b in range(local):
        lse = []
        for t in range(tiles):
            cols = pl.ds(b * span + t * LANES, LANES)
            part = rmax[:, cols]
            high = jnp.max(part, axis=0, keepdims=True)
            total = jnp.sum(rsum[:, cols] * jnp.exp2(part - high), axis=0, keepdims=True)
            lse.append(high + jnp.log2(total))

        def tops(step, _):
            for j in range(STEP):
                c = step * STEP + j
                best = [
                    bmax[c, :, pl.ds(b * span + t * LANES, LANES)] - lse[t] for t in range(tiles)
                ]
                top[b, c] = functools.reduce(jnp.maximum, best)
            return 0

        lax.fori_loop(0, blocks // STEP, tops, 0)
        best = jnp.max(top[b], axis=1)
        shift = group
        while shift < LANES:
            best = jnp.maximum(best, pltpu.roll(best, shift, 1))
            shift *= 2
        here_lanes = lane // group == b
        pooled = jnp.where(here_lanes, best, pooled)
        mine = jnp.where(here_lanes, order_ref[b].astype(F32), mine)
    valid = lane < width_q
    pooled = jnp.exp2(pooled)
    target = pooled / jnp.sum(pooled, axis=0, keepdims=True)

    gscale = gq_ref.shape[1] ** (-0.5)
    logits = product(kproj, qproj, NT) * gscale
    logits = jnp.where(ords[:, 0, :] > mine, MASKED, logits)
    shifted = logits - jnp.max(logits, axis=0, keepdims=True)
    weight = jnp.exp(shifted)
    norm = jnp.sum(weight, axis=0, keepdims=True)
    logp = shifted - jnp.log(norm)
    count = group * heads * blocks
    safe = jnp.log(jnp.where(target > 0, target, 1.0))
    terms = jnp.where((target > 0) & valid, target * (safe - logp), 0.0) * (1.0 / count)
    rowtot = jnp.sum(target, axis=0, keepdims=True)
    dlogit = jnp.where(valid, (weight / norm * rowtot - target) * (gscale / count), 0.0)
    share = LANES // width_q
    packed = blocks // share
    for v in range(packed // 8):
        rolled = [
            pltpu.roll(dlogit[(v * share + g) * 8:(v * share + g + 1) * 8], g * width_q, 1) if g else
            dlogit[v * share * 8:(v * share + 1) * 8]
            for g in range(share)
        ]
        mbuf[me, pl.ds(v * 8, 8), :] = functools.reduce(jnp.add, rolled)
    mbuf[me, pl.ds(packed, 8), :] = jnp.sum(terms.reshape(blocks // 8, 8, LANES), axis=0)

    def sum_copy(slot, k, to):
        return pltpu.make_async_remote_copy(
            src_ref=mbuf.at[slot], dst_ref=mbuf.at[slot], send_sem=msend.at[k], recv_sem=mrecv.at[slot],
            device_id={"seq": to}, device_id_type=MESH,
        )

    shares = [sum_copy(me, k, (me + k) % n) for k in range(1, n)]
    for copy in shares:
        copy.start()
    for k in range(1, n):
        sum_copy((me + k) % n, k, me).wait_recv()
    lbuf[head] = jnp.sum(mbuf[:, packed:, :], axis=0)

    def loss_copy(slot, k, to):
        return pltpu.make_async_remote_copy(
            src_ref=lbuf.at[slot], dst_ref=lbuf.at[slot], send_sem=lsend.at[k], recv_sem=lrecv.at[slot],
            device_id={"head": to}, device_id_type=MESH,
        )

    losses = [loss_copy(head, k, (head + k) % heads) for k in range(1, heads)]
    for copy in losses:
        copy.start()
    tiles_of = []
    for t in range(blocks // 8):
        chunks = []
        for first in range(0, n, share):
            chunk = jnp.zeros((8, LANES), F32)
            for g in range(share):
                piece = mbuf[first + g, pl.ds(t // share * 8, 8), :]
                if g != t % share:
                    piece = pltpu.roll(piece, (g - t % share) % share * width_q, 1)
                chunk = jnp.where(lane // width_q == g, piece, chunk)
            chunks.append(chunk)
        tiles_of.append(jnp.concatenate(chunks, axis=1))
    dlogits = jnp.concatenate(tiles_of, axis=0)
    queries = kbuf[:, tok + extra:, :].reshape(n * width_q, width)
    high, low = parts(dlogits)
    grad = jnp.dot(high, queries, preferred_element_type=F32) + jnp.dot(
        low, queries, preferred_element_type=F32
    )
    dq_ref[...] = product(grad, kproj, TN)
    dk_ref[...] = product(kpool, product(grad, gq_ref[...]), TN)
    for k in range(1, heads):
        loss_copy((head + k) % heads, k, head).wait_recv()
    loss = lbuf[0]
    for slot in range(1, heads):
        loss = loss + lbuf[slot]
    loss_ref[0, 0] = jnp.sum(loss)
    for copy in sends + forwards + shares + losses:
        copy.wait_send()


def solution(mesh):
    n, heads = mesh.shape["seq"], mesh.shape["head"]

    def shards(queries, keys, block_order, gate_query, gate_key):
        tok, group, width = queries.shape
        local = tok // BLOCK
        blocks = local * n
        extra = -(-4 * local // 16) * 16
        dim = gate_query.shape[2]
        pooled = gate_key.shape[1]
        vmem = pl.BlockSpec(memory_space=pltpu.VMEM)
        hbm = pl.BlockSpec(memory_space=pltpu.HBM)
        smem = pl.BlockSpec(memory_space=pltpu.SMEM)
        dma = pltpu.SemaphoreType.DMA
        block_rows = pltpu.VMEM((blocks, 8, width), F32)
        loss, grad_q, grad_k = pl.pallas_call(
            functools.partial(kernel, n, heads, group),
            out_shape=(
                jax.ShapeDtypeStruct((1, 1), F32),
                pltpu.VMEM((width, dim), F32),
                pltpu.VMEM((pooled, dim), F32),
            ),
            in_specs=[hbm] * 5,
            out_specs=(smem, vmem, vmem),
            scratch_shapes=[
                pltpu.VMEM((n, tok + extra + local * group, width), BF16),
                pltpu.VMEM((blocks, 8, tok * group), F32),
                pltpu.VMEM((8, tok * group), F32),
                pltpu.VMEM((8, tok * group), F32),
                block_rows,
                block_rows,
                block_rows,
                block_rows,
                pltpu.VMEM((local, blocks, 8, width), F32),
                pltpu.VMEM((n, blocks * local * group // LANES + 8, width), F32),
                pltpu.VMEM((heads, 8, width), F32),
                pltpu.SMEM((local,), jnp.int32),
                pltpu.VMEM((tok * group, width), BF16),
                pltpu.VMEM((width, tok * group), BF16),
                pltpu.VMEM((width, dim), BF16),
                pltpu.VMEM((pooled, dim), BF16),
                dma((n,)), dma((n,)), dma((n,)), dma((n,)), dma((n,)), dma((heads,)), dma((heads,)), dma((5,)),
            ],
            compiler_params=pltpu.CompilerParams(
                collective_id=0, has_side_effects=True, vmem_limit_bytes=48 << 20
            ),
        )(
            *(
                pltpu.with_memory_space_constraint(x, pltpu.HBM)
                for x in (
                    block_order,
                    queries.reshape(tok * group, width),
                    keys.reshape(tok, width),
                    gate_query[0],
                    gate_key[0],
                )
            )
        )
        return loss[0, 0], grad_q[None], grad_k[None]

    return jax.shard_map(
        shards,
        mesh=mesh,
        in_specs=(
            P("seq", "head", None),
            P("seq", "head", None),
            P("seq"),
            P("head", None, None),
            P("head", None, None),
        ),
        out_specs=(P(), P("head", None, None), P("head", None, None)),
        check_vma=False,
    )
```

```python
import functools
import math

import jax
import jax.numpy as jnp
from jax import lax
from jax.experimental import pallas as pl
from jax.experimental.pallas import tpu as pltpu
from jax.sharding import PartitionSpec as P

BLOCK = 64
MESH = pl.DeviceIdType.MESH
F32 = jnp.float32
BF16 = jnp.bfloat16
MASKED = -1e30
NT = (((1,), (1,)), ((), ()))
TN = (((0,), (0,)), ((), ()))
LANES = 128
STEP = 32


def parts(x):
    high = x.astype(BF16)
    return high, (x - high.astype(F32)).astype(BF16)


def product(x, y, dims=(((1,), (0,)), ((), ()))):
    (xc,), (yc,) = dims[0]
    xs = parts(x) if x.dtype == F32 else (x,)
    ys = parts(y) if y.dtype == F32 else (y,)
    pairs = [(i, j) for i in range(len(xs)) for j in range(len(ys)) if i + j < 2]
    left = jnp.concatenate([xs[i] for i, _ in pairs], axis=xc)
    right = jnp.concatenate([ys[j] for _, j in pairs], axis=yc)
    return lax.dot_general(left, right, dims, preferred_element_type=F32)


def kernel(
    n, heads, group, order_hbm, q_hbm, k_hbm, gq_hbm, gk_hbm,
    loss_ref, dq_ref, dk_ref,
    kbuf, bmax, rmax, rsum, ords, kmax, kmin, kmean, top, mbuf, lbuf,
    order_ref, q_ref, qt, gq_ref, gk_ref,
    csend, dsend, krecv, fsend, msend, mrecv, lsend, lrecv, held,
):
    tok, width = k_hbm.shape
    local = tok // BLOCK
    width_q = local * group
    extra = kbuf.shape[1] - tok - width_q
    blocks = n * local
    span = BLOCK * group
    far = n // 2
    k2 = width ** (-0.5) * math.log2(math.e)
    me = lax.axis_index("seq")
    head = lax.axis_index("head")
    a, r = me // 2, me % 2
    partner = a * 2 + (r + 1) % 2

    barrier = pltpu.get_barrier_semaphore()
    for k in range(1, n):
        pl.semaphore_signal(barrier, inc=1, device_id={"seq": (me + k) % n}, device_id_type=MESH)
    for k in range(1, heads):
        pl.semaphore_signal(barrier, inc=1, device_id={"head": (head + k) % heads}, device_id_type=MESH)

    fetch = [
        pltpu.make_async_copy(k_hbm, kbuf.at[me, pl.ds(0, tok), :], held.at[0]),
        pltpu.make_async_copy(order_hbm, order_ref, held.at[1]),
        pltpu.make_async_copy(q_hbm, q_ref, held.at[2]),
        pltpu.make_async_copy(gq_hbm, gq_ref, held.at[3]),
        pltpu.make_async_copy(gk_hbm, gk_ref, held.at[4]),
    ]
    for copy in fetch:
        copy.start()

    fetch[1].wait()
    fetch[0].wait()
    row = lax.broadcasted_iota(jnp.int32, (extra, width), 0)
    tail = jnp.zeros((extra, width), F32)
    for i in range(local):
        part = kbuf[me, pl.ds(i * BLOCK, BLOCK), :].astype(F32).reshape(BLOCK // 8, 8, width)
        pieces = (
            order_ref[i].astype(F32),
            jnp.max(jnp.max(part, axis=0), axis=0, keepdims=True),
            jnp.min(jnp.min(part, axis=0), axis=0, keepdims=True),
            jnp.sum(jnp.sum(part, axis=0), axis=0, keepdims=True) * (1.0 / BLOCK),
        )
        for m, piece in enumerate(pieces):
            tail = jnp.where(row == 4 * i + m, piece, tail)
    kbuf[me, pl.ds(tok, extra), :] = tail.astype(BF16)
    fetch[2].wait()
    qpool = [
        jnp.sum(
            q_ref[pl.ds(b * span, span), :].astype(F32).reshape(BLOCK, group, width), axis=0
        )
        for b in range(local)
    ]
    qp = (jnp.concatenate(qpool, axis=0) * (1.0 / BLOCK)).astype(BF16)
    kbuf[me, pl.ds(tok + extra, width_q), :] = qp
    pl.semaphore_wait(barrier, n - 1 + heads - 1)

    def key_copy(slot, send, to):
        return pltpu.make_async_remote_copy(
            src_ref=kbuf.at[slot], dst_ref=kbuf.at[slot], send_sem=send, recv_sem=krecv.at[slot],
            device_id={"seq": to}, device_id_type=MESH,
        )

    def onward(source, side):
        goes = (a + side >= 0) & (a + side < far) & ((a - source) * side >= 0)
        slot = source * 2 + r
        sem = csend.at[slot] if side > 0 else dsend.at[slot]
        return goes, key_copy(slot, sem, (a + side) * 2 + r)

    def across(source):
        slot = source * 2 + r
        return key_copy(slot, fsend.at[slot], partner)

    for side in (1, -1):
        goes, copy = onward(a, side)
        pl.when(goes)(copy.start)
    across(a).start()

    short = jnp.minimum(a, far - 1 - a)
    longer = jnp.where(a < far - 1 - a, 1, -1)

    def source_of(i):
        near = jnp.where(i % 2 == 1, a - (i + 1) // 2, a + (i + 1) // 2)
        return jnp.where(i <= 2 * short, near, a + longer * (i - short))

    for b in range(local):
        qt[:, pl.ds(b * span, span)] = q_ref[pl.ds(b * span, span), :].T
    fetch[3].wait()
    fetch[4].wait()
    qproj = jnp.dot(qp, gq_ref[...], preferred_element_type=F32)
    qproj = jnp.concatenate([qproj, jnp.zeros((LANES - width_q, qproj.shape[1]), F32)], axis=0)
    rmax[...] = jnp.full_like(rmax, MASKED)
    rsum[...] = jnp.zeros_like(rsum)

    half = span // 2

    ahead = lax.broadcasted_iota(jnp.int32, (BLOCK, half), 0) - (
        lax.broadcasted_iota(jnp.int32, (BLOCK, half), 1) // group
    )

    def wait_keys(slot):
        key_copy(slot, fsend.at[slot], partner).wait_recv()

    def shard(j, _):
        slot = source_of(j // 2) * 2 + (r + j) % 2
        step = (j + 1) // 2
        for side in (1, -1):
            source = a - side * step

            @pl.when((j % 2 == 1) & (source >= 0) & (source < far))
            def _():
                wait_keys(source * 2 + r)
                across(source).start()
                goes, copy = onward(source, side)
                pl.when(goes)(copy.start)

        @pl.when(j % 2 == 1)
        def _():
            wait_keys(slot)

        tail = kbuf[slot, pl.ds(tok, extra), :].astype(F32)
        for i in range(local):
            at = slot * local + i
            for m, ref in enumerate((ords, kmax, kmin, kmean)):
                ref[at] = jnp.broadcast_to(tail[4 * i + m:4 * i + m + 1], (8, width))
        unmasked = jnp.where(j == 0, 0, 2 * BLOCK)

        for b in range(local):
            here = order_ref[b].astype(F32)
            for part in range(2):
                cols = pl.ds(b * span + part * half, half)
                scores = jnp.dot(
                    kbuf[slot, pl.ds(0, tok), :], qt[:, cols], preferred_element_type=F32
                )
                highs, sums = [], []
                for i in range(local):
                    s = scores[i * BLOCK:(i + 1) * BLOCK]
                    if b == i:
                        s = jnp.where(ahead > unmasked + part * (BLOCK // 2), MASKED / k2, s)
                    s = s.reshape(BLOCK // 8, 8, half)
                    high = jnp.max(s, axis=0)
                    sums.append(jnp.sum(jnp.exp2((s - high) * k2), axis=0))
                    later = jnp.broadcast_to(tail[4 * i:4 * i + 1, :1], (8, half)) > here
                    high = jnp.where(later, MASKED, high * k2)
                    bmax[slot * local + i, :, cols] = high
                    highs.append(high)
                old = rmax[:, cols]
                new = functools.reduce(jnp.maximum, highs, old)
                total = rsum[:, cols] * jnp.exp2(old - new)
                for high, amount in zip(highs, sums):
                    total = total + amount * jnp.exp2(high - new)
                rmax[:, cols] = new
                rsum[:, cols] = total
        return 0

    lax.fori_loop(0, n, shard, 0)
    kpool = jnp.concatenate([ref[:, 0, :] for ref in (kmax, kmin, kmean)], axis=1).astype(BF16)
    kproj = jnp.dot(kpool, gk_ref[...], preferred_element_type=F32)

    lane = lax.broadcasted_iota(jnp.int32, (1, LANES), 1)
    tiles = span // LANES
    pooled = jnp.zeros((blocks, LANES), F32)
    mine = jnp.zeros((1, LANES), F32)
    for b in range(local):
        lse = []
        for t in range(tiles):
            cols = pl.ds(b * span + t * LANES, LANES)
            part = rmax[:, cols]
            high = jnp.max(part, axis=0, keepdims=True)
            total = jnp.sum(rsum[:, cols] * jnp.exp2(part - high), axis=0, keepdims=True)
            lse.append(high + jnp.log2(total))

        def tops(step, _):
            for j in range(STEP):
                c = step * STEP + j
                best = [
                    bmax[c, :, pl.ds(b * span + t * LANES, LANES)] - lse[t] for t in range(tiles)
                ]
                top[b, c] = functools.reduce(jnp.maximum, best)
            return 0

        lax.fori_loop(0, blocks // STEP, tops, 0)
        best = jnp.max(top[b], axis=1)
        shift = group
        while shift < LANES:
            best = jnp.maximum(best, pltpu.roll(best, shift, 1))
            shift *= 2
        here_lanes = lane // group == b
        pooled = jnp.where(here_lanes, best, pooled)
        mine = jnp.where(here_lanes, order_ref[b].astype(F32), mine)
    valid = lane < width_q
    pooled = jnp.exp2(pooled)
    target = pooled / jnp.sum(pooled, axis=0, keepdims=True)

    gscale = gq_ref.shape[1] ** (-0.5)
    logits = product(kproj, qproj, NT) * gscale
    logits = jnp.where(ords[:, 0, :] > mine, MASKED, logits)
    shifted = logits - jnp.max(logits, axis=0, keepdims=True)
    weight = jnp.exp(shifted)
    norm = jnp.sum(weight, axis=0, keepdims=True)
    logp = shifted - jnp.log(norm)
    count = group * heads * blocks
    safe = jnp.log(jnp.where(target > 0, target, 1.0))
    terms = jnp.where((target > 0) & valid, target * (safe - logp), 0.0) * (1.0 / count)
    rowtot = jnp.sum(target, axis=0, keepdims=True)
    dlogit = jnp.where(valid, (weight / norm * rowtot - target) * (gscale / count), 0.0)
    share = LANES // width_q
    packed = blocks // share
    for v in range(packed // 8):
        rolled = [
            pltpu.roll(dlogit[(v * share + g) * 8:(v * share + g + 1) * 8], g * width_q, 1) if g else
            dlogit[v * share * 8:(v * share + 1) * 8]
            for g in range(share)
        ]
        mbuf[me, pl.ds(v * 8, 8), :] = functools.reduce(jnp.add, rolled)
    mbuf[me, pl.ds(packed, 8), :] = jnp.sum(terms.reshape(blocks // 8, 8, LANES), axis=0)

    def sum_copy(slot, k, to):
        return pltpu.make_async_remote_copy(
            src_ref=mbuf.at[slot], dst_ref=mbuf.at[slot], send_sem=msend.at[k], recv_sem=mrecv.at[slot],
            device_id={"seq": to}, device_id_type=MESH,
        )

    shares = [sum_copy(me, k, (me + k) % n) for k in range(1, n)]
    for copy in shares:
        copy.start()
    for k in range(1, n):
        sum_copy((me + k) % n, k, me).wait_recv()
    lbuf[head] = jnp.sum(mbuf[:, packed:, :], axis=0)

    def loss_copy(slot, k, to):
        return pltpu.make_async_remote_copy(
            src_ref=lbuf.at[slot], dst_ref=lbuf.at[slot], send_sem=lsend.at[k], recv_sem=lrecv.at[slot],
            device_id={"head": to}, device_id_type=MESH,
        )

    losses = [loss_copy(head, k, (head + k) % heads) for k in range(1, heads)]
    for copy in losses:
        copy.start()
    tiles_of = []
    for t in range(blocks // 8):
        chunks = []
        for first in range(0, n, share):
            chunk = jnp.zeros((8, LANES), F32)
            for g in range(share):
                piece = mbuf[first + g, pl.ds(t // share * 8, 8), :]
                if g != t % share:
                    piece = pltpu.roll(piece, (g - t % share) % share * width_q, 1)
                chunk = jnp.where(lane // width_q == g, piece, chunk)
            chunks.append(chunk)
        tiles_of.append(jnp.concatenate(chunks, axis=1))
    dlogits = jnp.concatenate(tiles_of, axis=0)
    queries = kbuf[:, tok + extra:, :].reshape(n * width_q, width)
    high, low = parts(dlogits)
    grad = jnp.dot(high, queries, preferred_element_type=F32) + jnp.dot(
        low, queries, preferred_element_type=F32
    )
    dq_ref[...] = product(grad, kproj, TN)
    dk_ref[...] = product(kpool, product(grad, gq_ref[...]), TN)
    for k in range(1, heads):
        loss_copy((head + k) % heads, k, head).wait_recv()
    loss = lbuf[0]
    for slot in range(1, heads):
        loss = loss + lbuf[slot]
    loss_ref[0, 0] = jnp.sum(loss)
    for copy in shares + losses:
        copy.wait_send()

    def sent(source, _):
        across(source).wait_send()
        for side in (1, -1):
            goes, copy = onward(source, side)
            pl.when(goes)(copy.wait_send)
        return 0

    lax.fori_loop(0, far, sent, 0)


def solution(mesh):
    n, heads = mesh.shape["seq"], mesh.shape["head"]

    def shards(queries, keys, block_order, gate_query, gate_key):
        tok, group, width = queries.shape
        local = tok // BLOCK
        blocks = local * n
        extra = -(-4 * local // 16) * 16
        dim = gate_query.shape[2]
        pooled = gate_key.shape[1]
        vmem = pl.BlockSpec(memory_space=pltpu.VMEM)
        hbm = pl.BlockSpec(memory_space=pltpu.HBM)
        smem = pl.BlockSpec(memory_space=pltpu.SMEM)
        dma = pltpu.SemaphoreType.DMA
        block_rows = pltpu.VMEM((blocks, 8, width), F32)
        loss, grad_q, grad_k = pl.pallas_call(
            functools.partial(kernel, n, heads, group),
            out_shape=(
                jax.ShapeDtypeStruct((1, 1), F32),
                pltpu.VMEM((width, dim), F32),
                pltpu.VMEM((pooled, dim), F32),
            ),
            in_specs=[hbm] * 5,
            out_specs=(smem, vmem, vmem),
            scratch_shapes=[
                pltpu.VMEM((n, tok + extra + local * group, width), BF16),
                pltpu.VMEM((blocks, 8, tok * group), F32),
                pltpu.VMEM((8, tok * group), F32),
                pltpu.VMEM((8, tok * group), F32),
                block_rows,
                block_rows,
                block_rows,
                block_rows,
                pltpu.VMEM((local, blocks, 8, width), F32),
                pltpu.VMEM((n, blocks * local * group // LANES + 8, width), F32),
                pltpu.VMEM((heads, 8, width), F32),
                pltpu.SMEM((local,), jnp.int32),
                pltpu.VMEM((tok * group, width), BF16),
                pltpu.VMEM((width, tok * group), BF16),
                pltpu.VMEM((width, dim), BF16),
                pltpu.VMEM((pooled, dim), BF16),
                dma((n,)), dma((n,)), dma((n,)), dma((n,)), dma((n,)), dma((n,)), dma((heads,)), dma((heads,)), dma((5,)),
            ],
            compiler_params=pltpu.CompilerParams(
                collective_id=0, has_side_effects=True, vmem_limit_bytes=48 << 20
            ),
        )(
            *(
                pltpu.with_memory_space_constraint(x, pltpu.HBM)
                for x in (
                    block_order,
                    queries.reshape(tok * group, width),
                    keys.reshape(tok, width),
                    gate_query[0],
                    gate_key[0],
                )
            )
        )
        return loss[0, 0], grad_q[None], grad_k[None]

    return jax.shard_map(
        shards,
        mesh=mesh,
        in_specs=(
            P("seq", "head", None),
            P("seq", "head", None),
            P("seq"),
            P("head", None, None),
            P("head", None, None),
        ),
        out_specs=(P(), P("head", None, None), P("head", None, None)),
        check_vma=False,
    )
```

```python
import functools
import math

import jax
import jax.numpy as jnp
from jax import lax
from jax.experimental import pallas as pl
from jax.experimental.pallas import tpu as pltpu
from jax.sharding import PartitionSpec as P

BLOCK = 64
MESH = pl.DeviceIdType.MESH
F32 = jnp.float32
BF16 = jnp.bfloat16
MASKED = -1e30
NT = (((1,), (1,)), ((), ()))
TN = (((0,), (0,)), ((), ()))
LANES = 128
STEP = 32


def parts(x):
    high = x.astype(BF16)
    return high, (x - high.astype(F32)).astype(BF16)


def product(x, y, dims=(((1,), (0,)), ((), ()))):
    (xc,), (yc,) = dims[0]
    xs = parts(x) if x.dtype == F32 else (x,)
    ys = parts(y) if y.dtype == F32 else (y,)
    pairs = [(i, j) for i in range(len(xs)) for j in range(len(ys)) if i + j < 2]
    left = jnp.concatenate([xs[i] for i, _ in pairs], axis=xc)
    right = jnp.concatenate([ys[j] for _, j in pairs], axis=yc)
    return lax.dot_general(left, right, dims, preferred_element_type=F32)


def row_maxima(rows):
    at = lax.broadcasted_iota(jnp.int32, rows[0].shape, 0)
    shift = 4
    while shift:
        low = at % (2 * shift) < shift
        merged = []
        for x, y in zip(rows[:shift], rows[shift:]):
            keep, move = jnp.where(low, x, y), jnp.where(low, y, x)
            moved = pltpu.roll(move, shift, 0)
            if shift < 4:
                moved = jnp.where(low, pltpu.roll(move, 8 - shift, 0), moved)
            merged.append(jnp.maximum(keep, moved))
        rows = merged
        shift //= 2
    return rows[0]


def kernel(
    n, heads, group, order_hbm, q_hbm, k_hbm, gq_hbm, gk_hbm,
    loss_ref, dq_ref, dk_ref,
    kbuf, bmax, rmax, rsum, ords, kmax, kmin, kmean, top, scores, mbuf, lbuf,
    order_ref, q_ref, qt, gq_ref, gk_ref,
    ksend, krecv, fsend, msend, mrecv, lsend, lrecv, held,
):
    tok, width = k_hbm.shape
    local = tok // BLOCK
    width_q = local * group
    extra = kbuf.shape[1] - tok - width_q
    blocks = n * local
    span = BLOCK * group
    far = n // 2
    k2 = width ** (-0.5) * math.log2(math.e)
    me = lax.axis_index("seq")
    head = lax.axis_index("head")
    a, r = me // 2, me % 2
    partner = a * 2 + (r + 1) % 2

    barrier = pltpu.get_barrier_semaphore()
    for k in range(1, n):
        pl.semaphore_signal(barrier, inc=1, device_id={"seq": (me + k) % n}, device_id_type=MESH)
    for k in range(1, heads):
        pl.semaphore_signal(barrier, inc=1, device_id={"head": (head + k) % heads}, device_id_type=MESH)

    fetch = [
        pltpu.make_async_copy(k_hbm, kbuf.at[me, pl.ds(0, tok), :], held.at[0]),
        pltpu.make_async_copy(order_hbm, order_ref, held.at[1]),
        pltpu.make_async_copy(q_hbm, q_ref, held.at[2]),
        pltpu.make_async_copy(gq_hbm, gq_ref, held.at[3]),
        pltpu.make_async_copy(gk_hbm, gk_ref, held.at[4]),
    ]
    for copy in fetch:
        copy.start()

    fetch[1].wait()
    fetch[0].wait()
    row = lax.broadcasted_iota(jnp.int32, (extra, width), 0)
    tail = jnp.zeros((extra, width), F32)
    for i in range(local):
        part = kbuf[me, pl.ds(i * BLOCK, BLOCK), :].astype(F32).reshape(BLOCK // 8, 8, width)
        pieces = (
            order_ref[i].astype(F32),
            jnp.max(jnp.max(part, axis=0), axis=0, keepdims=True),
            jnp.min(jnp.min(part, axis=0), axis=0, keepdims=True),
            jnp.sum(jnp.sum(part, axis=0), axis=0, keepdims=True) * (1.0 / BLOCK),
        )
        for m, piece in enumerate(pieces):
            tail = jnp.where(row == 4 * i + m, piece, tail)
    kbuf[me, pl.ds(tok, extra), :] = tail.astype(BF16)
    fetch[2].wait()
    qpool = [
        jnp.sum(
            q_ref[pl.ds(b * span, span), :].astype(F32).reshape(BLOCK, group, width), axis=0
        )
        for b in range(local)
    ]
    qp = (jnp.concatenate(qpool, axis=0) * (1.0 / BLOCK)).astype(BF16)
    kbuf[me, pl.ds(tok + extra, width_q), :] = qp
    pl.semaphore_wait(barrier, n - 1 + heads - 1)

    def key_copy(slot, send, to):
        return pltpu.make_async_remote_copy(
            src_ref=kbuf.at[slot], dst_ref=kbuf.at[slot], send_sem=send, recv_sem=krecv.at[slot],
            device_id={"seq": to}, device_id_type=MESH,
        )

    sends = []
    for k in range(1, far):
        to = (a + k) % far * 2 + r
        sends.append(key_copy(me, ksend.at[k], to))
    sends.insert(1, key_copy(me, ksend.at[0], partner))
    for copy in sends:
        copy.start()

    for b in range(local):
        qt[:, pl.ds(b * span, span)] = q_ref[pl.ds(b * span, span), :].T
    fetch[3].wait()
    fetch[4].wait()
    qproj = jnp.dot(qp, gq_ref[...], preferred_element_type=F32)
    qproj = jnp.concatenate([qproj, jnp.zeros((LANES - width_q, qproj.shape[1]), F32)], axis=0)
    rmax[...] = jnp.full_like(rmax, MASKED)
    rsum[...] = jnp.zeros_like(rsum)

    half = span // 2

    ahead = lax.broadcasted_iota(jnp.int32, (BLOCK, LANES), 0) - (
        lax.broadcasted_iota(jnp.int32, (BLOCK, LANES), 1) // group
    )

    def wait_keys(slot):
        key_copy(slot, ksend.at[0], partner).wait_recv()

    def shard(j, _):
        back = j // 2
        slot = (a - back + far) % far * 2 + (r + j) % 2

        @pl.when((j % 2 == 1) & (back + 1 < far))
        def _():
            direct = (a - back - 1 + far) % far * 2 + r
            wait_keys(direct)
            key_copy(direct, fsend.at[back + 1], partner).start()

        @pl.when(j % 2 == 1)
        def _():
            wait_keys(slot)

        tail = kbuf[slot, pl.ds(tok, extra), :].astype(F32)
        for i in range(local):
            at = slot * local + i
            for m, ref in enumerate((ords, kmax, kmin, kmean)):
                ref[at] = jnp.broadcast_to(tail[4 * i + m:4 * i + m + 1], (8, width))
        unmasked = jnp.where(j == 0, 0, 2 * BLOCK)

        spread = [jnp.broadcast_to(tail[4 * i:4 * i + 1], (8, width)) for i in range(local)]

        def multiply(t):
            scores[t % 2] = jnp.dot(
                kbuf[slot, pl.ds(0, tok), :], qt[:, pl.ds(t * half, half)],
                preferred_element_type=F32,
            )

        count = 2 * local
        multiply(0)
        for t in range(count):
            if t + 1 < count:
                multiply(t + 1)
            b, part = t // 2, t % 2
            here = order_ref[b].astype(F32)
            for lanes in range(0, half, LANES):
                cols = pl.ds(t * half + lanes, LANES)
                highs, sums = [], []
                for i in range(local):
                    s = scores[t % 2, pl.ds(i * BLOCK, BLOCK), pl.ds(lanes, LANES)]
                    if b == i:
                        limit = unmasked + (part * half + lanes) // group
                        s = jnp.where(ahead > limit, MASKED / k2, s)
                    s = s.reshape(BLOCK // 8, 8, LANES)
                    high = jnp.max(s, axis=0)
                    sums.append(jnp.sum(jnp.exp2((s - high) * k2), axis=0))
                    high = jnp.where(spread[i] > here, MASKED, high * k2)
                    bmax[slot * local + i, :, cols] = high
                    highs.append(high)
                old = rmax[:, cols]
                new = functools.reduce(jnp.maximum, highs, old)
                total = rsum[:, cols] * jnp.exp2(old - new)
                for high, amount in zip(highs, sums):
                    total = total + amount * jnp.exp2(high - new)
                rmax[:, cols] = new
                rsum[:, cols] = total
        return 0

    lax.fori_loop(0, n, shard, 0)
    forwards = [
        key_copy((a - k + far) % far * 2 + r, fsend.at[k], partner) for k in range(1, far)
    ]

    kpool = jnp.concatenate([ref[:, 0, :] for ref in (kmax, kmin, kmean)], axis=1).astype(BF16)
    kproj = jnp.dot(kpool, gk_ref[...], preferred_element_type=F32)

    lane = lax.broadcasted_iota(jnp.int32, (1, LANES), 1)
    tiles = span // LANES
    pooled = jnp.zeros((blocks, LANES), F32)
    mine = jnp.zeros((1, LANES), F32)
    for b in range(local):
        lse = []
        for t in range(tiles):
            cols = pl.ds(b * span + t * LANES, LANES)
            part = rmax[:, cols]
            high = jnp.max(part, axis=0, keepdims=True)
            total = jnp.sum(rsum[:, cols] * jnp.exp2(part - high), axis=0, keepdims=True)
            lse.append(high + jnp.log2(total))

        def tops(step, _):
            for eight in range(STEP // 8):
                first = pl.multiple_of(step * STEP + eight * 8, 8)
                rows = []
                for j in range(8):
                    best = [
                        bmax[first + j, :, pl.ds(b * span + t * LANES, LANES)] - lse[t]
                        for t in range(tiles)
                    ]
                    rows.append(functools.reduce(jnp.maximum, best))
                top[b, pl.ds(first, 8), :] = row_maxima(rows)
            return 0

        lax.fori_loop(0, blocks // STEP, tops, 0)
        best = top[b]
        shift = group
        while shift < LANES:
            best = jnp.maximum(best, pltpu.roll(best, shift, 1))
            shift *= 2
        here_lanes = lane // group == b
        pooled = jnp.where(here_lanes, best, pooled)
        mine = jnp.where(here_lanes, order_ref[b].astype(F32), mine)
    valid = lane < width_q
    pooled = jnp.exp2(pooled)
    target = pooled / jnp.sum(pooled, axis=0, keepdims=True)

    gscale = gq_ref.shape[1] ** (-0.5)
    logits = product(kproj, qproj, NT) * gscale
    logits = jnp.where(ords[:, 0, :] > mine, MASKED, logits)
    shifted = logits - jnp.max(logits, axis=0, keepdims=True)
    weight = jnp.exp(shifted)
    norm = jnp.sum(weight, axis=0, keepdims=True)
    logp = shifted - jnp.log(norm)
    count = group * heads * blocks
    safe = jnp.log(jnp.where(target > 0, target, 1.0))
    terms = jnp.where((target > 0) & valid, target * (safe - logp), 0.0) * (1.0 / count)
    rowtot = jnp.sum(target, axis=0, keepdims=True)
    dlogit = jnp.where(valid, (weight / norm * rowtot - target) * (gscale / count), 0.0)
    share = LANES // width_q
    packed = blocks // share
    for v in range(packed // 8):
        rolled = [
            pltpu.roll(dlogit[(v * share + g) * 8:(v * share + g + 1) * 8], g * width_q, 1) if g else
            dlogit[v * share * 8:(v * share + 1) * 8]
            for g in range(share)
        ]
        mbuf[me, pl.ds(v * 8, 8), :] = functools.reduce(jnp.add, rolled)
    mbuf[me, pl.ds(packed, 8), :] = jnp.sum(terms.reshape(blocks // 8, 8, LANES), axis=0)

    def sum_copy(slot, k, to):
        return pltpu.make_async_remote_copy(
            src_ref=mbuf.at[slot], dst_ref=mbuf.at[slot], send_sem=msend.at[k], recv_sem=mrecv.at[slot],
            device_id={"seq": to}, device_id_type=MESH,
        )

    shares = [sum_copy(me, k, (me + k) % n) for k in range(1, n)]
    for copy in shares:
        copy.start()
    for k in range(1, n):
        sum_copy((me + k) % n, k, me).wait_recv()
    lbuf[head] = jnp.sum(mbuf[:, packed:, :], axis=0)

    def loss_copy(slot, k, to):
        return pltpu.make_async_remote_copy(
            src_ref=lbuf.at[slot], dst_ref=lbuf.at[slot], send_sem=lsend.at[k], recv_sem=lrecv.at[slot],
            device_id={"head": to}, device_id_type=MESH,
        )

    losses = [loss_copy(head, k, (head + k) % heads) for k in range(1, heads)]
    for copy in losses:
        copy.start()
    tiles_of = []
    for t in range(blocks // 8):
        chunks = []
        for first in range(0, n, share):
            chunk = jnp.zeros((8, LANES), F32)
            for g in range(share):
                piece = mbuf[first + g, pl.ds(t // share * 8, 8), :]
                if g != t % share:
                    piece = pltpu.roll(piece, (g - t % share) % share * width_q, 1)
                chunk = jnp.where(lane // width_q == g, piece, chunk)
            chunks.append(chunk)
        tiles_of.append(jnp.concatenate(chunks, axis=1))
    dlogits = jnp.concatenate(tiles_of, axis=0)
    queries = kbuf[:, tok + extra:, :].reshape(n * width_q, width)
    high, low = parts(dlogits)
    grad = jnp.dot(high, queries, preferred_element_type=F32) + jnp.dot(
        low, queries, preferred_element_type=F32
    )
    dq_ref[...] = product(grad, kproj, TN)
    dk_ref[...] = product(kpool, product(grad, gq_ref[...]), TN)
    for k in range(1, heads):
        loss_copy((head + k) % heads, k, head).wait_recv()
    loss = lbuf[0]
    for slot in range(1, heads):
        loss = loss + lbuf[slot]
    loss_ref[0, 0] = jnp.sum(loss)
    for copy in sends + forwards + shares + losses:
        copy.wait_send()


def solution(mesh):
    n, heads = mesh.shape["seq"], mesh.shape["head"]

    def shards(queries, keys, block_order, gate_query, gate_key):
        tok, group, width = queries.shape
        local = tok // BLOCK
        blocks = local * n
        extra = -(-4 * local // 16) * 16
        dim = gate_query.shape[2]
        pooled = gate_key.shape[1]
        vmem = pl.BlockSpec(memory_space=pltpu.VMEM)
        hbm = pl.BlockSpec(memory_space=pltpu.HBM)
        smem = pl.BlockSpec(memory_space=pltpu.SMEM)
        dma = pltpu.SemaphoreType.DMA
        block_rows = pltpu.VMEM((blocks, 8, width), F32)
        loss, grad_q, grad_k = pl.pallas_call(
            functools.partial(kernel, n, heads, group),
            out_shape=(
                jax.ShapeDtypeStruct((1, 1), F32),
                pltpu.VMEM((width, dim), F32),
                pltpu.VMEM((pooled, dim), F32),
            ),
            in_specs=[hbm] * 5,
            out_specs=(smem, vmem, vmem),
            scratch_shapes=[
                pltpu.VMEM((n, tok + extra + local * group, width), BF16),
                pltpu.VMEM((blocks, 8, tok * group), F32),
                pltpu.VMEM((8, tok * group), F32),
                pltpu.VMEM((8, tok * group), F32),
                block_rows,
                block_rows,
                block_rows,
                block_rows,
                pltpu.VMEM((local, blocks, width), F32),
                pltpu.VMEM((2, tok, BLOCK * group // 2), F32),
                pltpu.VMEM((n, blocks * local * group // LANES + 8, width), F32),
                pltpu.VMEM((heads, 8, width), F32),
                pltpu.SMEM((local,), jnp.int32),
                pltpu.VMEM((tok * group, width), BF16),
                pltpu.VMEM((width, tok * group), BF16),
                pltpu.VMEM((width, dim), BF16),
                pltpu.VMEM((pooled, dim), BF16),
                dma((n,)), dma((n,)), dma((n,)), dma((n,)), dma((n,)), dma((heads,)), dma((heads,)), dma((5,)),
            ],
            compiler_params=pltpu.CompilerParams(
                collective_id=0, has_side_effects=True, vmem_limit_bytes=48 << 20
            ),
        )(
            *(
                pltpu.with_memory_space_constraint(x, pltpu.HBM)
                for x in (
                    block_order,
                    queries.reshape(tok * group, width),
                    keys.reshape(tok, width),
                    gate_query[0],
                    gate_key[0],
                )
            )
        )
        return loss[0, 0], grad_q[None], grad_k[None]

    return jax.shard_map(
        shards,
        mesh=mesh,
        in_specs=(
            P("seq", "head", None),
            P("seq", "head", None),
            P("seq"),
            P("head", None, None),
            P("head", None, None),
        ),
        out_specs=(P(), P("head", None, None), P("head", None, None)),
        check_vma=False,
    )
```

```python
import functools
import math

import jax
import jax.numpy as jnp
from jax import lax
from jax.experimental import pallas as pl
from jax.experimental.pallas import tpu as pltpu
from jax.sharding import PartitionSpec as P

BLOCK = 64
MESH = pl.DeviceIdType.MESH
F32 = jnp.float32
BF16 = jnp.bfloat16
MASKED = -1e30
NT = (((1,), (1,)), ((), ()))
TN = (((0,), (0,)), ((), ()))
LANES = 128
STEP = 32


def parts(x):
    high = x.astype(BF16)
    return high, (x - high.astype(F32)).astype(BF16)


def product(x, y, dims=(((1,), (0,)), ((), ()))):
    (xc,), (yc,) = dims[0]
    xs = parts(x) if x.dtype == F32 else (x,)
    ys = parts(y) if y.dtype == F32 else (y,)
    pairs = [(i, j) for i in range(len(xs)) for j in range(len(ys)) if i + j < 2]
    left = jnp.concatenate([xs[i] for i, _ in pairs], axis=xc)
    right = jnp.concatenate([ys[j] for _, j in pairs], axis=yc)
    return lax.dot_general(left, right, dims, preferred_element_type=F32)


def row_maxima(rows):
    at = lax.broadcasted_iota(jnp.int32, rows[0].shape, 0)
    shift = 4
    while shift:
        low = at % (2 * shift) < shift
        merged = []
        for x, y in zip(rows[:shift], rows[shift:]):
            keep, move = jnp.where(low, x, y), jnp.where(low, y, x)
            moved = pltpu.roll(move, shift, 0)
            if shift < 4:
                moved = jnp.where(low, pltpu.roll(move, 8 - shift, 0), moved)
            merged.append(jnp.maximum(keep, moved))
        rows = merged
        shift //= 2
    return rows[0]


def kernel(
    n, heads, group, order_hbm, q_hbm, k_hbm, gq_hbm, gk_hbm,
    loss_ref, dq_ref, dk_ref,
    kbuf, bmax, rmax, rsum, ords, kmax, kmin, kmean, top, scores, mbuf, lbuf,
    order_ref, q_ref, qt, gq_ref, gk_ref,
    ksend, krecv, fsend, msend, mrecv, lsend, lrecv, held,
):
    tok, width = k_hbm.shape
    local = tok // BLOCK
    width_q = local * group
    extra = kbuf.shape[1] - tok - width_q
    blocks = n * local
    span = BLOCK * group
    far = n // 2
    k2 = width ** (-0.5) * math.log2(math.e)
    me = lax.axis_index("seq")
    head = lax.axis_index("head")
    a, r = me // 2, me % 2
    partner = a * 2 + (r + 1) % 2

    barrier = pltpu.get_barrier_semaphore()
    for k in range(1, n):
        pl.semaphore_signal(barrier, inc=1, device_id={"seq": (me + k) % n}, device_id_type=MESH)
    for k in range(1, heads):
        pl.semaphore_signal(barrier, inc=1, device_id={"head": (head + k) % heads}, device_id_type=MESH)

    fetch = [
        pltpu.make_async_copy(k_hbm, kbuf.at[me, pl.ds(0, tok), :], held.at[0]),
        pltpu.make_async_copy(order_hbm, order_ref, held.at[1]),
        pltpu.make_async_copy(q_hbm, q_ref, held.at[2]),
        pltpu.make_async_copy(gq_hbm, gq_ref, held.at[3]),
        pltpu.make_async_copy(gk_hbm, gk_ref, held.at[4]),
    ]
    for copy in fetch:
        copy.start()

    fetch[1].wait()
    fetch[0].wait()
    row = lax.broadcasted_iota(jnp.int32, (extra, width), 0)
    tail = jnp.zeros((extra, width), F32)
    for i in range(local):
        part = kbuf[me, pl.ds(i * BLOCK, BLOCK), :].astype(F32).reshape(BLOCK // 8, 8, width)
        pieces = (
            order_ref[i].astype(F32),
            jnp.max(jnp.max(part, axis=0), axis=0, keepdims=True),
            jnp.min(jnp.min(part, axis=0), axis=0, keepdims=True),
            jnp.sum(jnp.sum(part, axis=0), axis=0, keepdims=True) * (1.0 / BLOCK),
        )
        for m, piece in enumerate(pieces):
            tail = jnp.where(row == 4 * i + m, piece, tail)
    kbuf[me, pl.ds(tok, extra), :] = tail.astype(BF16)
    fetch[2].wait()
    qpool = [
        jnp.sum(
            q_ref[pl.ds(b * span, span), :].astype(F32).reshape(BLOCK, group, width), axis=0
        )
        for b in range(local)
    ]
    qp = (jnp.concatenate(qpool, axis=0) * (1.0 / BLOCK)).astype(BF16)
    kbuf[me, pl.ds(tok + extra, width_q), :] = qp
    pl.semaphore_wait(barrier, n - 1 + heads - 1)

    def key_copy(slot, send, to):
        return pltpu.make_async_remote_copy(
            src_ref=kbuf.at[slot], dst_ref=kbuf.at[slot], send_sem=send, recv_sem=krecv.at[slot],
            device_id={"seq": to}, device_id_type=MESH,
        )

    sends = []
    for k in range(1, far):
        to = (a + k) % far * 2 + r
        sends.append(key_copy(me, ksend.at[k], to))
    sends.insert(1, key_copy(me, ksend.at[0], partner))
    for copy in sends:
        copy.start()

    for b in range(local):
        qt[:, pl.ds(b * span, span)] = q_ref[pl.ds(b * span, span), :].T
    fetch[3].wait()
    fetch[4].wait()
    qproj = jnp.dot(qp, gq_ref[...], preferred_element_type=F32)
    qproj = jnp.concatenate([qproj, jnp.zeros((LANES - width_q, qproj.shape[1]), F32)], axis=0)
    rmax[...] = jnp.full_like(rmax, MASKED)
    rsum[...] = jnp.zeros_like(rsum)

    half = span // 2

    ahead = lax.broadcasted_iota(jnp.int32, (BLOCK, LANES), 0) - (
        lax.broadcasted_iota(jnp.int32, (BLOCK, LANES), 1) // group
    )

    def wait_keys(slot):
        key_copy(slot, ksend.at[0], partner).wait_recv()

    def shard(j, _):
        back = j // 2
        slot = (a - back + far) % far * 2 + (r + j) % 2

        @pl.when((j % 2 == 1) & (back + 1 < far))
        def _():
            direct = (a - back - 1 + far) % far * 2 + r
            wait_keys(direct)
            key_copy(direct, fsend.at[back + 1], partner).start()

        @pl.when(j % 2 == 1)
        def _():
            wait_keys(slot)

        tail = kbuf[slot, pl.ds(tok, extra), :].astype(F32)
        for i in range(local):
            at = slot * local + i
            for m, ref in enumerate((ords, kmax, kmin, kmean)):
                ref[at] = jnp.broadcast_to(tail[4 * i + m:4 * i + m + 1], (8, width))
        unmasked = jnp.where(j == 0, 0, 2 * BLOCK)

        spread = [jnp.broadcast_to(tail[4 * i:4 * i + 1], (8, width)) for i in range(local)]

        def multiply(t):
            scores[t % 2] = jnp.dot(
                kbuf[slot, pl.ds(0, tok), :], qt[:, pl.ds(t * half, half)],
                preferred_element_type=F32,
            )

        count = 2 * local
        multiply(0)
        for t in range(count):
            if t + 1 < count:
                multiply(t + 1)
            b, part = t // 2, t % 2
            here = order_ref[b].astype(F32)
            for lanes in range(0, half, LANES):
                cols = pl.ds(t * half + lanes, LANES)
                highs, sums = [], []
                for i in range(local):
                    s = scores[t % 2, pl.ds(i * BLOCK, BLOCK), pl.ds(lanes, LANES)]
                    if b == i:
                        limit = unmasked + (part * half + lanes) // group
                        s = jnp.where(ahead > limit, MASKED / k2, s)
                    s = s.reshape(BLOCK // 8, 8, LANES)
                    high = jnp.max(s, axis=0)
                    power = jnp.exp2(((s - high) * k2).astype(BF16).reshape(BLOCK, LANES))
                    half_sums = [power[w:w + 16] for w in range(0, BLOCK, 16)]
                    while len(half_sums) > 1:
                        half_sums = [u + v for u, v in zip(half_sums[::2], half_sums[1::2])]
                    pair_sum = half_sums[0].astype(F32)
                    sums.append(pair_sum[:8] + pair_sum[8:])
                    high = jnp.where(spread[i] > here, MASKED, high * k2)
                    bmax[slot * local + i, :, cols] = high
                    highs.append(high)
                old = rmax[:, cols]
                new = functools.reduce(jnp.maximum, highs, old)
                total = rsum[:, cols] * jnp.exp2(old - new)
                for high, amount in zip(highs, sums):
                    total = total + amount * jnp.exp2(high - new)
                rmax[:, cols] = new
                rsum[:, cols] = total
        return 0

    lax.fori_loop(0, n, shard, 0)
    forwards = [
        key_copy((a - k + far) % far * 2 + r, fsend.at[k], partner) for k in range(1, far)
    ]

    kpool = jnp.concatenate([ref[:, 0, :] for ref in (kmax, kmin, kmean)], axis=1).astype(BF16)
    kproj = jnp.dot(kpool, gk_ref[...], preferred_element_type=F32)

    lane = lax.broadcasted_iota(jnp.int32, (1, LANES), 1)
    tiles = span // LANES
    pooled = jnp.zeros((blocks, LANES), F32)
    mine = jnp.zeros((1, LANES), F32)
    for b in range(local):
        lse = []
        for t in range(tiles):
            cols = pl.ds(b * span + t * LANES, LANES)
            part = rmax[:, cols]
            high = jnp.max(part, axis=0, keepdims=True)
            total = jnp.sum(rsum[:, cols] * jnp.exp2(part - high), axis=0, keepdims=True)
            lse.append(high + jnp.log2(total))

        def tops(step, _):
            for eight in range(STEP // 8):
                first = pl.multiple_of(step * STEP + eight * 8, 8)
                rows = []
                for j in range(8):
                    best = [
                        bmax[first + j, :, pl.ds(b * span + t * LANES, LANES)] - lse[t]
                        for t in range(tiles)
                    ]
                    rows.append(functools.reduce(jnp.maximum, best))
                top[b, pl.ds(first, 8), :] = row_maxima(rows)
            return 0

        lax.fori_loop(0, blocks // STEP, tops, 0)
        best = top[b]
        shift = group
        while shift < LANES:
            best = jnp.maximum(best, pltpu.roll(best, shift, 1))
            shift *= 2
        here_lanes = lane // group == b
        pooled = jnp.where(here_lanes, best, pooled)
        mine = jnp.where(here_lanes, order_ref[b].astype(F32), mine)
    valid = lane < width_q
    pooled = jnp.exp2(pooled)
    target = pooled / jnp.sum(pooled, axis=0, keepdims=True)

    gscale = gq_ref.shape[1] ** (-0.5)
    logits = product(kproj, qproj, NT) * gscale
    logits = jnp.where(ords[:, 0, :] > mine, MASKED, logits)
    shifted = logits - jnp.max(logits, axis=0, keepdims=True)
    weight = jnp.exp(shifted)
    norm = jnp.sum(weight, axis=0, keepdims=True)
    logp = shifted - jnp.log(norm)
    count = group * heads * blocks
    safe = jnp.log(jnp.where(target > 0, target, 1.0))
    terms = jnp.where((target > 0) & valid, target * (safe - logp), 0.0) * (1.0 / count)
    rowtot = jnp.sum(target, axis=0, keepdims=True)
    dlogit = jnp.where(valid, (weight / norm * rowtot - target) * (gscale / count), 0.0)
    share = LANES // width_q
    packed = blocks // share
    for v in range(packed // 8):
        rolled = [
            pltpu.roll(dlogit[(v * share + g) * 8:(v * share + g + 1) * 8], g * width_q, 1) if g else
            dlogit[v * share * 8:(v * share + 1) * 8]
            for g in range(share)
        ]
        mbuf[me, pl.ds(v * 8, 8), :] = functools.reduce(jnp.add, rolled)
    mbuf[me, pl.ds(packed, 8), :] = jnp.sum(terms.reshape(blocks // 8, 8, LANES), axis=0)

    def sum_copy(slot, k, to):
        return pltpu.make_async_remote_copy(
            src_ref=mbuf.at[slot], dst_ref=mbuf.at[slot], send_sem=msend.at[k], recv_sem=mrecv.at[slot],
            device_id={"seq": to}, device_id_type=MESH,
        )

    shares = [sum_copy(me, k, (me + k) % n) for k in range(1, n)]
    for copy in shares:
        copy.start()
    for k in range(1, n):
        sum_copy((me + k) % n, k, me).wait_recv()
    lbuf[head] = jnp.sum(mbuf[:, packed:, :], axis=0)

    def loss_copy(slot, k, to):
        return pltpu.make_async_remote_copy(
            src_ref=lbuf.at[slot], dst_ref=lbuf.at[slot], send_sem=lsend.at[k], recv_sem=lrecv.at[slot],
            device_id={"head": to}, device_id_type=MESH,
        )

    losses = [loss_copy(head, k, (head + k) % heads) for k in range(1, heads)]
    for copy in losses:
        copy.start()
    tiles_of = []
    for t in range(blocks // 8):
        chunks = []
        for first in range(0, n, share):
            chunk = jnp.zeros((8, LANES), F32)
            for g in range(share):
                piece = mbuf[first + g, pl.ds(t // share * 8, 8), :]
                if g != t % share:
                    piece = pltpu.roll(piece, (g - t % share) % share * width_q, 1)
                chunk = jnp.where(lane // width_q == g, piece, chunk)
            chunks.append(chunk)
        tiles_of.append(jnp.concatenate(chunks, axis=1))
    dlogits = jnp.concatenate(tiles_of, axis=0)
    queries = kbuf[:, tok + extra:, :].reshape(n * width_q, width)
    high, low = parts(dlogits)
    grad = jnp.dot(high, queries, preferred_element_type=F32) + jnp.dot(
        low, queries, preferred_element_type=F32
    )
    dq_ref[...] = product(grad, kproj, TN)
    dk_ref[...] = product(kpool, product(grad, gq_ref[...]), TN)
    for k in range(1, heads):
        loss_copy((head + k) % heads, k, head).wait_recv()
    loss = lbuf[0]
    for slot in range(1, heads):
        loss = loss + lbuf[slot]
    loss_ref[0, 0] = jnp.sum(loss)
    for copy in sends + forwards + shares + losses:
        copy.wait_send()


def solution(mesh):
    n, heads = mesh.shape["seq"], mesh.shape["head"]

    def shards(queries, keys, block_order, gate_query, gate_key):
        tok, group, width = queries.shape
        local = tok // BLOCK
        blocks = local * n
        extra = -(-4 * local // 16) * 16
        dim = gate_query.shape[2]
        pooled = gate_key.shape[1]
        vmem = pl.BlockSpec(memory_space=pltpu.VMEM)
        hbm = pl.BlockSpec(memory_space=pltpu.HBM)
        smem = pl.BlockSpec(memory_space=pltpu.SMEM)
        dma = pltpu.SemaphoreType.DMA
        block_rows = pltpu.VMEM((blocks, 8, width), F32)
        loss, grad_q, grad_k = pl.pallas_call(
            functools.partial(kernel, n, heads, group),
            out_shape=(
                jax.ShapeDtypeStruct((1, 1), F32),
                pltpu.VMEM((width, dim), F32),
                pltpu.VMEM((pooled, dim), F32),
            ),
            in_specs=[hbm] * 5,
            out_specs=(smem, vmem, vmem),
            scratch_shapes=[
                pltpu.VMEM((n, tok + extra + local * group, width), BF16),
                pltpu.VMEM((blocks, 8, tok * group), F32),
                pltpu.VMEM((8, tok * group), F32),
                pltpu.VMEM((8, tok * group), F32),
                block_rows,
                block_rows,
                block_rows,
                block_rows,
                pltpu.VMEM((local, blocks, width), F32),
                pltpu.VMEM((2, tok, BLOCK * group // 2), F32),
                pltpu.VMEM((n, blocks * local * group // LANES + 8, width), F32),
                pltpu.VMEM((heads, 8, width), F32),
                pltpu.SMEM((local,), jnp.int32),
                pltpu.VMEM((tok * group, width), BF16),
                pltpu.VMEM((width, tok * group), BF16),
                pltpu.VMEM((width, dim), BF16),
                pltpu.VMEM((pooled, dim), BF16),
                dma((n,)), dma((n,)), dma((n,)), dma((n,)), dma((n,)), dma((heads,)), dma((heads,)), dma((5,)),
            ],
            compiler_params=pltpu.CompilerParams(
                collective_id=0, has_side_effects=True, vmem_limit_bytes=48 << 20
            ),
        )(
            *(
                pltpu.with_memory_space_constraint(x, pltpu.HBM)
                for x in (
                    block_order,
                    queries.reshape(tok * group, width),
                    keys.reshape(tok, width),
                    gate_query[0],
                    gate_key[0],
                )
            )
        )
        return loss[0, 0], grad_q[None], grad_k[None]

    return jax.shard_map(
        shards,
        mesh=mesh,
        in_specs=(
            P("seq", "head", None),
            P("seq", "head", None),
            P("seq"),
            P("head", None, None),
            P("head", None, None),
        ),
        out_specs=(P(), P("head", None, None), P("head", None, None)),
        check_vma=False,
    )
```

```python
import functools
import math

import jax
import jax.numpy as jnp
from jax import lax
from jax.experimental import pallas as pl
from jax.experimental.pallas import tpu as pltpu
from jax.sharding import PartitionSpec as P

BLOCK = 64
MESH = pl.DeviceIdType.MESH
F32 = jnp.float32
BF16 = jnp.bfloat16
MASKED = -1e30
NT = (((1,), (1,)), ((), ()))
TN = (((0,), (0,)), ((), ()))
LANES = 128
STEP = 32


def parts(x):
    high = x.astype(BF16)
    return high, (x - high.astype(F32)).astype(BF16)


def product(x, y, dims=(((1,), (0,)), ((), ()))):
    (xc,), (yc,) = dims[0]
    xs = parts(x) if x.dtype == F32 else (x,)
    ys = parts(y) if y.dtype == F32 else (y,)
    pairs = [(i, j) for i in range(len(xs)) for j in range(len(ys)) if i + j < 2]
    left = jnp.concatenate([xs[i] for i, _ in pairs], axis=xc)
    right = jnp.concatenate([ys[j] for _, j in pairs], axis=yc)
    return lax.dot_general(left, right, dims, preferred_element_type=F32)


def row_maxima(rows):
    at = lax.broadcasted_iota(jnp.int32, rows[0].shape, 0)
    shift = 4
    while shift:
        low = at % (2 * shift) < shift
        merged = []
        for x, y in zip(rows[:shift], rows[shift:]):
            keep, move = jnp.where(low, x, y), jnp.where(low, y, x)
            moved = pltpu.roll(move, shift, 0)
            if shift < 4:
                moved = jnp.where(low, pltpu.roll(move, 8 - shift, 0), moved)
            merged.append(jnp.maximum(keep, moved))
        rows = merged
        shift //= 2
    return rows[0]


def kernel(
    n, heads, group, order_hbm, q_hbm, k_hbm, gq_hbm, gk_hbm,
    loss_ref, dq_ref, dk_ref,
    kbuf, bmax, rmax, rsum, ords, kmax, kmin, kmean, top, scores, mbuf, lbuf,
    order_ref, q_ref, qt, gq_ref, gk_ref,
    ksend, krecv, fsend, msend, mrecv, lsend, lrecv, held,
):
    tok, width = k_hbm.shape
    local = tok // BLOCK
    width_q = local * group
    extra = kbuf.shape[1] // 2 - tok - width_q
    side = extra + width_q
    blocks = n * local
    span = BLOCK * group
    far = n // 2
    k2 = width ** (-0.5) * math.log2(math.e)
    me = lax.axis_index("seq")
    head = lax.axis_index("head")
    a, r = me // 2, me % 2
    keys_at = pl.multiple_of(side + r * tok, 16)
    side_at = pl.multiple_of(r * (side + 2 * tok), 16)
    partner = a * 2 + (r + 1) % 2

    barrier = pltpu.get_barrier_semaphore()
    for k in range(1, n):
        pl.semaphore_signal(barrier, inc=1, device_id={"seq": (me + k) % n}, device_id_type=MESH)
    for k in range(1, heads):
        pl.semaphore_signal(barrier, inc=1, device_id={"head": (head + k) % heads}, device_id_type=MESH)

    fetch = [
        pltpu.make_async_copy(k_hbm, kbuf.at[a, pl.ds(keys_at, tok), :], held.at[0]),
        pltpu.make_async_copy(order_hbm, order_ref, held.at[1]),
        pltpu.make_async_copy(q_hbm, q_ref, held.at[2]),
        pltpu.make_async_copy(gq_hbm, gq_ref, held.at[3]),
        pltpu.make_async_copy(gk_hbm, gk_ref, held.at[4]),
    ]
    for copy in fetch:
        copy.start()

    fetch[1].wait()
    fetch[0].wait()
    row = lax.broadcasted_iota(jnp.int32, (extra, width), 0)
    tail = jnp.zeros((extra, width), F32)
    for i in range(local):
        part = kbuf[a, pl.ds(pl.multiple_of(keys_at + i * BLOCK, 16), BLOCK), :].astype(F32).reshape(BLOCK // 8, 8, width)
        pieces = (
            order_ref[i].astype(F32),
            jnp.max(jnp.max(part, axis=0), axis=0, keepdims=True),
            jnp.min(jnp.min(part, axis=0), axis=0, keepdims=True),
            jnp.sum(jnp.sum(part, axis=0), axis=0, keepdims=True) * (1.0 / BLOCK),
        )
        for m, piece in enumerate(pieces):
            tail = jnp.where(row == 4 * i + m, piece, tail)
    kbuf[a, pl.ds(side_at, extra), :] = tail.astype(BF16)
    fetch[2].wait()
    qpool = [
        jnp.sum(
            q_ref[pl.ds(b * span, span), :].astype(F32).reshape(BLOCK, group, width), axis=0
        )
        for b in range(local)
    ]
    qp = (jnp.concatenate(qpool, axis=0) * (1.0 / BLOCK)).astype(BF16)
    kbuf[a, pl.ds(pl.multiple_of(side_at + extra, 16), width_q), :] = qp
    pl.semaphore_wait(barrier, n - 1 + heads - 1)

    def key_copy(slot, send, to):
        rows = pl.ds(pl.multiple_of(slot % 2 * (side + tok), 16), side + tok)
        at = slot // 2
        return pltpu.make_async_remote_copy(
            src_ref=kbuf.at[at, rows], dst_ref=kbuf.at[at, rows], send_sem=send, recv_sem=krecv.at[slot],
            device_id={"seq": to}, device_id_type=MESH,
        )

    sends = []
    for k in range(1, far):
        to = (a + k) % far * 2 + r
        sends.append(key_copy(me, ksend.at[k], to))
    sends.insert(1, key_copy(me, ksend.at[0], partner))
    for copy in sends:
        copy.start()

    for b in range(local):
        qt[:, pl.ds(b * span, span)] = q_ref[pl.ds(b * span, span), :].T
    fetch[3].wait()
    fetch[4].wait()
    qproj = jnp.dot(qp, gq_ref[...], preferred_element_type=F32)
    qproj = jnp.concatenate([qproj, jnp.zeros((LANES - width_q, qproj.shape[1]), F32)], axis=0)
    rmax[...] = jnp.full_like(rmax, MASKED)
    rsum[...] = jnp.zeros_like(rsum)

    half = span // 2

    ahead = lax.broadcasted_iota(jnp.int32, (BLOCK, LANES), 0) - (
        lax.broadcasted_iota(jnp.int32, (BLOCK, LANES), 1) // group
    )

    def wait_keys(slot):
        key_copy(slot, ksend.at[0], partner).wait_recv()

    def shards(k, _):
        line = (a - k + far) % far
        wait_keys(line * 2 + (r + 1) % 2)
        spread = []
        for p in range(2):
            tail = kbuf[line, pl.ds(p * (side + 2 * tok), extra), :].astype(F32)
            for i in range(local):
                at = line * 2 * local + p * local + i
                for m, ref in enumerate((ords, kmax, kmin, kmean)):
                    ref[at] = jnp.broadcast_to(tail[4 * i + m:4 * i + m + 1], (8, width))
                spread.append(jnp.broadcast_to(tail[4 * i:4 * i + 1], (8, width)))
        unmasked = [jnp.where((k == 0) & (r == p), 0, 2 * BLOCK) for p in range(2)]

        def multiply(t):
            scores[t % 2] = jnp.dot(
                kbuf[line, pl.ds(side, 2 * tok), :], qt[:, pl.ds(t * half, half)],
                preferred_element_type=F32,
            )

        count = 2 * local
        multiply(0)
        for t in range(count):
            if t == count // 2:
                @pl.when(k + 1 < far)
                def _():
                    direct = (a - k - 1 + far) % far * 2 + r
                    wait_keys(direct)
                    key_copy(direct, fsend.at[k + 1], partner).start()
            if t + 1 < count:
                multiply(t + 1)
            b, part = t // 2, t % 2
            here = order_ref[b].astype(F32)
            for lanes in range(0, half, LANES):
                cols = pl.ds(t * half + lanes, LANES)
                highs, sums = [], []
                for i in range(2 * local):
                    s = scores[t % 2, pl.ds(i * BLOCK, BLOCK), pl.ds(lanes, LANES)]
                    if b == i % local:
                        limit = unmasked[i // local] + (part * half + lanes) // group
                        s = jnp.where(ahead > limit, MASKED / k2, s)
                    s = s.reshape(BLOCK // 8, 8, LANES)
                    high = jnp.max(s, axis=0)
                    sums.append(jnp.sum(jnp.exp2((s - high) * k2), axis=0))
                    high = jnp.where(spread[i] > here, MASKED, high * k2)
                    bmax[line * 2 * local + i, :, cols] = high
                    highs.append(high)
                old = rmax[:, cols]
                new = functools.reduce(jnp.maximum, highs, old)
                total = rsum[:, cols] * jnp.exp2(old - new)
                for high, amount in zip(highs, sums):
                    total = total + amount * jnp.exp2(high - new)
                rmax[:, cols] = new
                rsum[:, cols] = total
        return 0

    lax.fori_loop(0, far, shards, 0)
    forwards = [
        key_copy((a - k + far) % far * 2 + r, fsend.at[k], partner) for k in range(1, far)
    ]

    kpool = jnp.concatenate([ref[:, 0, :] for ref in (kmax, kmin, kmean)], axis=1).astype(BF16)
    kproj = jnp.dot(kpool, gk_ref[...], preferred_element_type=F32)

    lane = lax.broadcasted_iota(jnp.int32, (1, LANES), 1)
    tiles = span // LANES
    pooled = jnp.zeros((blocks, LANES), F32)
    mine = jnp.zeros((1, LANES), F32)
    for b in range(local):
        lse = []
        for t in range(tiles):
            cols = pl.ds(b * span + t * LANES, LANES)
            part = rmax[:, cols]
            high = jnp.max(part, axis=0, keepdims=True)
            total = jnp.sum(rsum[:, cols] * jnp.exp2(part - high), axis=0, keepdims=True)
            lse.append(high + jnp.log2(total))

        def tops(step, _):
            for eight in range(STEP // 8):
                first = pl.multiple_of(step * STEP + eight * 8, 8)
                rows = []
                for j in range(8):
                    best = [
                        bmax[first + j, :, pl.ds(b * span + t * LANES, LANES)] - lse[t]
                        for t in range(tiles)
                    ]
                    rows.append(functools.reduce(jnp.maximum, best))
                top[b, pl.ds(first, 8), :] = row_maxima(rows)
            return 0

        lax.fori_loop(0, blocks // STEP, tops, 0)
        best = top[b]
        shift = group
        while shift < LANES:
            best = jnp.maximum(best, pltpu.roll(best, shift, 1))
            shift *= 2
        here_lanes = lane // group == b
        pooled = jnp.where(here_lanes, best, pooled)
        mine = jnp.where(here_lanes, order_ref[b].astype(F32), mine)
    valid = lane < width_q
    pooled = jnp.exp2(pooled)
    target = pooled / jnp.sum(pooled, axis=0, keepdims=True)

    gscale = gq_ref.shape[1] ** (-0.5)
    logits = product(kproj, qproj, NT) * gscale
    logits = jnp.where(ords[:, 0, :] > mine, MASKED, logits)
    shifted = logits - jnp.max(logits, axis=0, keepdims=True)
    weight = jnp.exp(shifted)
    norm = jnp.sum(weight, axis=0, keepdims=True)
    logp = shifted - jnp.log(norm)
    count = group * heads * blocks
    safe = jnp.log(jnp.where(target > 0, target, 1.0))
    terms = jnp.where((target > 0) & valid, target * (safe - logp), 0.0) * (1.0 / count)
    rowtot = jnp.sum(target, axis=0, keepdims=True)
    dlogit = jnp.where(valid, (weight / norm * rowtot - target) * (gscale / count), 0.0)
    share = LANES // width_q
    packed = blocks // share
    for v in range(packed // 8):
        rolled = [
            pltpu.roll(dlogit[(v * share + g) * 8:(v * share + g + 1) * 8], g * width_q, 1) if g else
            dlogit[v * share * 8:(v * share + 1) * 8]
            for g in range(share)
        ]
        mbuf[me, pl.ds(v * 8, 8), :] = functools.reduce(jnp.add, rolled)
    mbuf[me, pl.ds(packed, 8), :] = jnp.sum(terms.reshape(blocks // 8, 8, LANES), axis=0)

    def sum_copy(slot, k, to):
        return pltpu.make_async_remote_copy(
            src_ref=mbuf.at[slot], dst_ref=mbuf.at[slot], send_sem=msend.at[k], recv_sem=mrecv.at[slot],
            device_id={"seq": to}, device_id_type=MESH,
        )

    shares = [sum_copy(me, k, (me + k) % n) for k in range(1, n)]
    for copy in shares:
        copy.start()
    for k in range(1, n):
        sum_copy((me + k) % n, k, me).wait_recv()
    lbuf[head] = jnp.sum(mbuf[:, packed:, :], axis=0)

    def loss_copy(slot, k, to):
        return pltpu.make_async_remote_copy(
            src_ref=lbuf.at[slot], dst_ref=lbuf.at[slot], send_sem=lsend.at[k], recv_sem=lrecv.at[slot],
            device_id={"head": to}, device_id_type=MESH,
        )

    losses = [loss_copy(head, k, (head + k) % heads) for k in range(1, heads)]
    for copy in losses:
        copy.start()
    tiles_of = []
    for t in range(blocks // 8):
        chunks = []
        for first in range(0, n, share):
            chunk = jnp.zeros((8, LANES), F32)
            for g in range(share):
                piece = mbuf[first + g, pl.ds(t // share * 8, 8), :]
                if g != t % share:
                    piece = pltpu.roll(piece, (g - t % share) % share * width_q, 1)
                chunk = jnp.where(lane // width_q == g, piece, chunk)
            chunks.append(chunk)
        tiles_of.append(jnp.concatenate(chunks, axis=1))
    dlogits = jnp.concatenate(tiles_of, axis=0)
    queries = jnp.concatenate(
        [
            kbuf[slot // 2, pl.ds(slot % 2 * (side + 2 * tok) + extra, width_q), :]
            for slot in range(n)
        ],
        axis=0,
    )
    high, low = parts(dlogits)
    grad = jnp.dot(high, queries, preferred_element_type=F32) + jnp.dot(
        low, queries, preferred_element_type=F32
    )
    dq_ref[...] = product(grad, kproj, TN)
    dk_ref[...] = product(kpool, product(grad, gq_ref[...]), TN)
    for k in range(1, heads):
        loss_copy((head + k) % heads, k, head).wait_recv()
    loss = lbuf[0]
    for slot in range(1, heads):
        loss = loss + lbuf[slot]
    loss_ref[0, 0] = jnp.sum(loss)
    for copy in sends + forwards + shares + losses:
        copy.wait_send()


def solution(mesh):
    n, heads = mesh.shape["seq"], mesh.shape["head"]

    def shards(queries, keys, block_order, gate_query, gate_key):
        tok, group, width = queries.shape
        local = tok // BLOCK
        blocks = local * n
        extra = -(-4 * local // 16) * 16
        dim = gate_query.shape[2]
        pooled = gate_key.shape[1]
        vmem = pl.BlockSpec(memory_space=pltpu.VMEM)
        hbm = pl.BlockSpec(memory_space=pltpu.HBM)
        smem = pl.BlockSpec(memory_space=pltpu.SMEM)
        dma = pltpu.SemaphoreType.DMA
        block_rows = pltpu.VMEM((blocks, 8, width), F32)
        loss, grad_q, grad_k = pl.pallas_call(
            functools.partial(kernel, n, heads, group),
            out_shape=(
                jax.ShapeDtypeStruct((1, 1), F32),
                pltpu.VMEM((width, dim), F32),
                pltpu.VMEM((pooled, dim), F32),
            ),
            in_specs=[hbm] * 5,
            out_specs=(smem, vmem, vmem),
            scratch_shapes=[
                pltpu.VMEM((n // 2, 2 * (tok + extra + local * group), width), BF16),
                pltpu.VMEM((blocks, 8, tok * group), F32),
                pltpu.VMEM((8, tok * group), F32),
                pltpu.VMEM((8, tok * group), F32),
                block_rows,
                block_rows,
                block_rows,
                block_rows,
                pltpu.VMEM((local, blocks, width), F32),
                pltpu.VMEM((2, 2 * tok, BLOCK * group // 2), F32),
                pltpu.VMEM((n, blocks * local * group // LANES + 8, width), F32),
                pltpu.VMEM((heads, 8, width), F32),
                pltpu.SMEM((local,), jnp.int32),
                pltpu.VMEM((tok * group, width), BF16),
                pltpu.VMEM((width, tok * group), BF16),
                pltpu.VMEM((width, dim), BF16),
                pltpu.VMEM((pooled, dim), BF16),
                dma((n,)), dma((n,)), dma((n,)), dma((n,)), dma((n,)), dma((heads,)), dma((heads,)), dma((5,)),
            ],
            compiler_params=pltpu.CompilerParams(
                collective_id=0, has_side_effects=True, vmem_limit_bytes=48 << 20
            ),
        )(
            *(
                pltpu.with_memory_space_constraint(x, pltpu.HBM)
                for x in (
                    block_order,
                    queries.reshape(tok * group, width),
                    keys.reshape(tok, width),
                    gate_query[0],
                    gate_key[0],
                )
            )
        )
        return loss[0, 0], grad_q[None], grad_k[None]

    return jax.shard_map(
        shards,
        mesh=mesh,
        in_specs=(
            P("seq", "head", None),
            P("seq", "head", None),
            P("seq"),
            P("head", None, None),
            P("head", None, None),
        ),
        out_specs=(P(), P("head", None, None), P("head", None, None)),
        check_vma=False,
    )
```

```python
import functools
import math

import jax
import jax.numpy as jnp
from jax import lax
from jax.experimental import pallas as pl
from jax.experimental.pallas import tpu as pltpu
from jax.sharding import PartitionSpec as P

BLOCK = 64
MESH = pl.DeviceIdType.MESH
F32 = jnp.float32
BF16 = jnp.bfloat16
MASKED = -1e30
NT = (((1,), (1,)), ((), ()))
TN = (((0,), (0,)), ((), ()))
LANES = 128
STEP = 32


def parts(x):
    high = x.astype(BF16)
    return high, (x - high.astype(F32)).astype(BF16)


def product(x, y, dims=(((1,), (0,)), ((), ()))):
    (xc,), (yc,) = dims[0]
    xs = parts(x) if x.dtype == F32 else (x,)
    ys = parts(y) if y.dtype == F32 else (y,)
    pairs = [(i, j) for i in range(len(xs)) for j in range(len(ys)) if i + j < 2]
    left = jnp.concatenate([xs[i] for i, _ in pairs], axis=xc)
    right = jnp.concatenate([ys[j] for _, j in pairs], axis=yc)
    return lax.dot_general(left, right, dims, preferred_element_type=F32)


def row_maxima(rows):
    at = lax.broadcasted_iota(jnp.int32, rows[0].shape, 0)
    shift = 4
    while shift:
        low = at % (2 * shift) < shift
        merged = []
        for x, y in zip(rows[:shift], rows[shift:]):
            keep, move = jnp.where(low, x, y), jnp.where(low, y, x)
            moved = pltpu.roll(move, shift, 0)
            if shift < 4:
                moved = jnp.where(low, pltpu.roll(move, 8 - shift, 0), moved)
            merged.append(jnp.maximum(keep, moved))
        rows = merged
        shift //= 2
    return rows[0]


def kernel(
    n, heads, group, order_hbm, q_hbm, k_hbm, gq_hbm, gk_hbm,
    loss_ref, dq_ref, dk_ref,
    kbuf, bmax, rmax, rsum, ords, kmax, kmin, kmean, top, scores, mbuf, lbuf,
    order_ref, q_ref, qt, gq_ref, gk_ref,
    ksend, krecv, msend, mrecv, lsend, lrecv, held,
):
    tok, width = k_hbm.shape
    local = tok // BLOCK
    width_q = local * group
    extra = kbuf.shape[1] - tok - width_q
    blocks = n * local
    span = BLOCK * group
    far = n // 2
    k2 = width ** (-0.5) * math.log2(math.e)
    me = lax.axis_index("seq")
    head = lax.axis_index("head")
    a, r = me // 2, me % 2
    partner = a * 2 + (r + 1) % 2

    barrier = pltpu.get_barrier_semaphore()
    for k in range(1, n):
        pl.semaphore_signal(barrier, inc=1, device_id={"seq": (me + k) % n}, device_id_type=MESH)
    for k in range(1, heads):
        pl.semaphore_signal(barrier, inc=1, device_id={"head": (head + k) % heads}, device_id_type=MESH)

    fetch = [
        pltpu.make_async_copy(k_hbm, kbuf.at[me, pl.ds(0, tok), :], held.at[0]),
        pltpu.make_async_copy(order_hbm, order_ref, held.at[1]),
        pltpu.make_async_copy(q_hbm, q_ref, held.at[2]),
        pltpu.make_async_copy(gq_hbm, gq_ref, held.at[3]),
        pltpu.make_async_copy(gk_hbm, gk_ref, held.at[4]),
    ]
    for copy in fetch:
        copy.start()

    fetch[1].wait()
    fetch[0].wait()
    row = lax.broadcasted_iota(jnp.int32, (extra, width), 0)
    tail = jnp.zeros((extra, width), F32)
    for i in range(local):
        part = kbuf[me, pl.ds(i * BLOCK, BLOCK), :].astype(F32).reshape(BLOCK // 8, 8, width)
        pieces = (
            order_ref[i].astype(F32),
            jnp.max(jnp.max(part, axis=0), axis=0, keepdims=True),
            jnp.min(jnp.min(part, axis=0), axis=0, keepdims=True),
            jnp.sum(jnp.sum(part, axis=0), axis=0, keepdims=True) * (1.0 / BLOCK),
        )
        for m, piece in enumerate(pieces):
            tail = jnp.where(row == 4 * i + m, piece, tail)
    kbuf[me, pl.ds(tok, extra), :] = tail.astype(BF16)
    fetch[2].wait()
    qpool = [
        jnp.sum(
            q_ref[pl.ds(b * span, span), :].astype(F32).reshape(BLOCK, group, width), axis=0
        )
        for b in range(local)
    ]
    qp = (jnp.concatenate(qpool, axis=0) * (1.0 / BLOCK)).astype(BF16)
    kbuf[me, pl.ds(tok + extra, width_q), :] = qp
    pl.semaphore_wait(barrier, n - 1 + heads - 1)

    def key_copy(slot, send, to):
        return pltpu.make_async_remote_copy(
            src_ref=kbuf.at[slot], dst_ref=kbuf.at[slot], send_sem=send, recv_sem=krecv.at[slot],
            device_id={"seq": to}, device_id_type=MESH,
        )

    sends = [
        key_copy(me, ksend.at[j], (a + j // 2) % far * 2 + (r + j) % 2) for j in range(1, n)
    ]
    for copy in sends:
        copy.start()

    for b in range(local):
        qt[:, pl.ds(b * span, span)] = q_ref[pl.ds(b * span, span), :].T
    fetch[3].wait()
    fetch[4].wait()
    qproj = jnp.dot(qp, gq_ref[...], preferred_element_type=F32)
    qproj = jnp.concatenate([qproj, jnp.zeros((LANES - width_q, qproj.shape[1]), F32)], axis=0)
    rmax[...] = jnp.full_like(rmax, MASKED)
    rsum[...] = jnp.zeros_like(rsum)

    half = span // 2

    ahead = lax.broadcasted_iota(jnp.int32, (BLOCK, LANES), 0) - (
        lax.broadcasted_iota(jnp.int32, (BLOCK, LANES), 1) // group
    )

    def wait_keys(slot):
        key_copy(slot, ksend.at[0], partner).wait_recv()

    def shard(j, _):
        back = j // 2
        slot = (a - back + far) % far * 2 + (r + j) % 2

        @pl.when(j > 0)
        def _():
            wait_keys(slot)

        tail = kbuf[slot, pl.ds(tok, extra), :].astype(F32)
        for i in range(local):
            at = slot * local + i
            for m, ref in enumerate((ords, kmax, kmin, kmean)):
                ref[at] = jnp.broadcast_to(tail[4 * i + m:4 * i + m + 1], (8, width))
        unmasked = jnp.where(j == 0, 0, 2 * BLOCK)

        spread = [jnp.broadcast_to(tail[4 * i:4 * i + 1], (8, width)) for i in range(local)]

        def multiply(t):
            scores[t % 2] = jnp.dot(
                kbuf[slot, pl.ds(0, tok), :], qt[:, pl.ds(t * half, half)],
                preferred_element_type=F32,
            )

        count = 2 * local
        multiply(0)
        for t in range(count):
            if t + 1 < count:
                multiply(t + 1)
            b, part = t // 2, t % 2
            here = order_ref[b].astype(F32)
            for lanes in range(0, half, LANES):
                cols = pl.ds(t * half + lanes, LANES)
                highs, sums = [], []
                for i in range(local):
                    s = scores[t % 2, pl.ds(i * BLOCK, BLOCK), pl.ds(lanes, LANES)]
                    if b == i:
                        limit = unmasked + (part * half + lanes) // group
                        s = jnp.where(ahead > limit, MASKED / k2, s)
                    s = s.reshape(BLOCK // 8, 8, LANES)
                    high = jnp.max(s, axis=0)
                    sums.append(jnp.sum(jnp.exp2((s - high) * k2), axis=0))
                    high = jnp.where(spread[i] > here, MASKED, high * k2)
                    bmax[slot * local + i, :, cols] = high
                    highs.append(high)
                old = rmax[:, cols]
                new = functools.reduce(jnp.maximum, highs, old)
                total = rsum[:, cols] * jnp.exp2(old - new)
                for high, amount in zip(highs, sums):
                    total = total + amount * jnp.exp2(high - new)
                rmax[:, cols] = new
                rsum[:, cols] = total
        return 0

    lax.fori_loop(0, n, shard, 0)
    kpool = jnp.concatenate([ref[:, 0, :] for ref in (kmax, kmin, kmean)], axis=1).astype(BF16)
    kproj = jnp.dot(kpool, gk_ref[...], preferred_element_type=F32)

    lane = lax.broadcasted_iota(jnp.int32, (1, LANES), 1)
    tiles = span // LANES
    pooled = jnp.zeros((blocks, LANES), F32)
    mine = jnp.zeros((1, LANES), F32)
    for b in range(local):
        lse = []
        for t in range(tiles):
            cols = pl.ds(b * span + t * LANES, LANES)
            part = rmax[:, cols]
            high = jnp.max(part, axis=0, keepdims=True)
            total = jnp.sum(rsum[:, cols] * jnp.exp2(part - high), axis=0, keepdims=True)
            lse.append(high + jnp.log2(total))

        def tops(step, _):
            for eight in range(STEP // 8):
                first = pl.multiple_of(step * STEP + eight * 8, 8)
                rows = []
                for j in range(8):
                    best = [
                        bmax[first + j, :, pl.ds(b * span + t * LANES, LANES)] - lse[t]
                        for t in range(tiles)
                    ]
                    rows.append(functools.reduce(jnp.maximum, best))
                top[b, pl.ds(first, 8), :] = row_maxima(rows)
            return 0

        lax.fori_loop(0, blocks // STEP, tops, 0)
        best = top[b]
        shift = group
        while shift < LANES:
            best = jnp.maximum(best, pltpu.roll(best, shift, 1))
            shift *= 2
        here_lanes = lane // group == b
        pooled = jnp.where(here_lanes, best, pooled)
        mine = jnp.where(here_lanes, order_ref[b].astype(F32), mine)
    valid = lane < width_q
    pooled = jnp.exp2(pooled)
    target = pooled / jnp.sum(pooled, axis=0, keepdims=True)

    gscale = gq_ref.shape[1] ** (-0.5)
    logits = product(kproj, qproj, NT) * gscale
    logits = jnp.where(ords[:, 0, :] > mine, MASKED, logits)
    shifted = logits - jnp.max(logits, axis=0, keepdims=True)
    weight = jnp.exp(shifted)
    norm = jnp.sum(weight, axis=0, keepdims=True)
    logp = shifted - jnp.log(norm)
    count = group * heads * blocks
    safe = jnp.log(jnp.where(target > 0, target, 1.0))
    terms = jnp.where((target > 0) & valid, target * (safe - logp), 0.0) * (1.0 / count)
    rowtot = jnp.sum(target, axis=0, keepdims=True)
    dlogit = jnp.where(valid, (weight / norm * rowtot - target) * (gscale / count), 0.0)
    share = LANES // width_q
    packed = blocks // share
    for v in range(packed // 8):
        rolled = [
            pltpu.roll(dlogit[(v * share + g) * 8:(v * share + g + 1) * 8], g * width_q, 1) if g else
            dlogit[v * share * 8:(v * share + 1) * 8]
            for g in range(share)
        ]
        mbuf[me, pl.ds(v * 8, 8), :] = functools.reduce(jnp.add, rolled)
    mbuf[me, pl.ds(packed, 8), :] = jnp.sum(terms.reshape(blocks // 8, 8, LANES), axis=0)

    def sum_copy(slot, k, to):
        return pltpu.make_async_remote_copy(
            src_ref=mbuf.at[slot], dst_ref=mbuf.at[slot], send_sem=msend.at[k], recv_sem=mrecv.at[slot],
            device_id={"seq": to}, device_id_type=MESH,
        )

    shares = [sum_copy(me, k, (me + k) % n) for k in range(1, n)]
    for copy in shares:
        copy.start()
    for k in range(1, n):
        sum_copy((me + k) % n, k, me).wait_recv()
    lbuf[head] = jnp.sum(mbuf[:, packed:, :], axis=0)

    def loss_copy(slot, k, to):
        return pltpu.make_async_remote_copy(
            src_ref=lbuf.at[slot], dst_ref=lbuf.at[slot], send_sem=lsend.at[k], recv_sem=lrecv.at[slot],
            device_id={"head": to}, device_id_type=MESH,
        )

    losses = [loss_copy(head, k, (head + k) % heads) for k in range(1, heads)]
    for copy in losses:
        copy.start()
    tiles_of = []
    for t in range(blocks // 8):
        chunks = []
        for first in range(0, n, share):
            chunk = jnp.zeros((8, LANES), F32)
            for g in range(share):
                piece = mbuf[first + g, pl.ds(t // share * 8, 8), :]
                if g != t % share:
                    piece = pltpu.roll(piece, (g - t % share) % share * width_q, 1)
                chunk = jnp.where(lane // width_q == g, piece, chunk)
            chunks.append(chunk)
        tiles_of.append(jnp.concatenate(chunks, axis=1))
    dlogits = jnp.concatenate(tiles_of, axis=0)
    queries = kbuf[:, tok + extra:, :].reshape(n * width_q, width)
    high, low = parts(dlogits)
    grad = jnp.dot(high, queries, preferred_element_type=F32) + jnp.dot(
        low, queries, preferred_element_type=F32
    )
    dq_ref[...] = product(grad, kproj, TN)
    dk_ref[...] = product(kpool, product(grad, gq_ref[...]), TN)
    for k in range(1, heads):
        loss_copy((head + k) % heads, k, head).wait_recv()
    loss = lbuf[0]
    for slot in range(1, heads):
        loss = loss + lbuf[slot]
    loss_ref[0, 0] = jnp.sum(loss)
    for copy in sends + shares + losses:
        copy.wait_send()


def solution(mesh):
    n, heads = mesh.shape["seq"], mesh.shape["head"]

    def shards(queries, keys, block_order, gate_query, gate_key):
        tok, group, width = queries.shape
        local = tok // BLOCK
        blocks = local * n
        extra = -(-4 * local // 16) * 16
        dim = gate_query.shape[2]
        pooled = gate_key.shape[1]
        vmem = pl.BlockSpec(memory_space=pltpu.VMEM)
        hbm = pl.BlockSpec(memory_space=pltpu.HBM)
        smem = pl.BlockSpec(memory_space=pltpu.SMEM)
        dma = pltpu.SemaphoreType.DMA
        block_rows = pltpu.VMEM((blocks, 8, width), F32)
        loss, grad_q, grad_k = pl.pallas_call(
            functools.partial(kernel, n, heads, group),
            out_shape=(
                jax.ShapeDtypeStruct((1, 1), F32),
                pltpu.VMEM((width, dim), F32),
                pltpu.VMEM((pooled, dim), F32),
            ),
            in_specs=[hbm] * 5,
            out_specs=(smem, vmem, vmem),
            scratch_shapes=[
                pltpu.VMEM((n, tok + extra + local * group, width), BF16),
                pltpu.VMEM((blocks, 8, tok * group), F32),
                pltpu.VMEM((8, tok * group), F32),
                pltpu.VMEM((8, tok * group), F32),
                block_rows,
                block_rows,
                block_rows,
                block_rows,
                pltpu.VMEM((local, blocks, width), F32),
                pltpu.VMEM((2, tok, BLOCK * group // 2), F32),
                pltpu.VMEM((n, blocks * local * group // LANES + 8, width), F32),
                pltpu.VMEM((heads, 8, width), F32),
                pltpu.SMEM((local,), jnp.int32),
                pltpu.VMEM((tok * group, width), BF16),
                pltpu.VMEM((width, tok * group), BF16),
                pltpu.VMEM((width, dim), BF16),
                pltpu.VMEM((pooled, dim), BF16),
                dma((n,)), dma((n,)), dma((n,)), dma((n,)), dma((heads,)), dma((heads,)), dma((5,)),
            ],
            compiler_params=pltpu.CompilerParams(
                collective_id=0, has_side_effects=True, vmem_limit_bytes=48 << 20
            ),
        )(
            *(
                pltpu.with_memory_space_constraint(x, pltpu.HBM)
                for x in (
                    block_order,
                    queries.reshape(tok * group, width),
                    keys.reshape(tok, width),
                    gate_query[0],
                    gate_key[0],
                )
            )
        )
        return loss[0, 0], grad_q[None], grad_k[None]

    return jax.shard_map(
        shards,
        mesh=mesh,
        in_specs=(
            P("seq", "head", None),
            P("seq", "head", None),
            P("seq"),
            P("head", None, None),
            P("head", None, None),
        ),
        out_specs=(P(), P("head", None, None), P("head", None, None)),
        check_vma=False,
    )
```
